256 devices in a mesh: dp: 32 (over x, z), ctx: 8 (over y, core).
Axes of the slice: x: 4, y: 4, z: 8, core: 2. Of those that a mesh axis runs over, the one named last changes fastest.
Arguments:
- inputs: bfloat16 [32, 1024, 2048], P('dp', 'ctx'), may hold values from -12 to 12
- doc_ids: int32 [32, 1024], P('dp', 'ctx'), may hold values from 0 to 3, never falling along the last dimension, each value on 1 to 512 neighbouring positions
- dilation: int32 [1], replicated, may hold values from 1 to 256
- filter_w: bfloat16 [2, 2048, 2048], P(None, 'dp', 'ctx'), may hold values from -0.09375 to 0.09375
- gate_w: bfloat16 [2, 2048, 2048], P(None, 'dp', 'ctx'), may hold values from -0.09375 to 0.09375
- filter_m: float32 [2, 2048, 2048], P(None, 'dp', 'ctx'), may hold values from -0.01171875 to 0.01171875
- filter_v: float32 [2, 2048, 2048], P(None, 'dp', 'ctx'), may hold values from 1e-07 to 4e-06
- gate_m: float32 [2, 2048, 2048], P(None, 'dp', 'ctx'), may hold values from -0.01171875 to 0.01171875
- gate_v: float32 [2, 2048, 2048], P(None, 'dp', 'ctx'), may hold values from 1e-07 to 4e-06
- cotangent: bfloat16 [32, 1024, 2048], P('dp', 'ctx'), may hold values from -6 to 6
Outputs:
- layer_out: bfloat16 [32, 1024, 2048], P('dp', 'ctx')
- input_grad: bfloat16 [32, 1024, 2048], P('dp', 'ctx')
- new_filter_w: bfloat16 [2, 2048, 2048], P(None, 'dp', 'ctx')
- new_gate_w: bfloat16 [2, 2048, 2048], P(None, 'dp', 'ctx')
- new_filter_m: float32 [2, 2048, 2048], P(None, 'dp', 'ctx')
- new_filter_v: float32 [2, 2048, 2048], P(None, 'dp', 'ctx')
- new_gate_m: float32 [2, 2048, 2048], P(None, 'dp', 'ctx')
- new_gate_v: float32 [2, 2048, 2048], P(None, 'dp', 'ctx')
The draws below stay inside these ranges and needn't reach their ends.
Inputs may be any that keep to these rules, and one draw needn't show every extreme that they name: `doc_ids`: document numbers never fall along a sequence; a document covers at most 512 positions.
All inputs are finite; a program needn't handle non-finite values.
Results may differ from the reference program's by a relative error of at most 0.0075.
Values may be sent and summed in bfloat16 or wider, within the bound.
A program may use at most 128 MiB of HBM per device.

```python
import math
import jax
import jax.numpy as jnp
import numpy as np
from jax import lax

C = 2048
TD = 128
STEP = 10
LEN = 1024
BATCH = 32
TOKENS = 32768


def raised(result, key, source, target, shards_of, factor):
    owner, partner = [(jnp.arange(result.shape[position]) // (result.shape[position] // shards_of)).reshape([-1 if axis == position else 1 for axis in range(result.ndim)]) for position in (source, target)]
    chosen = jax.random.permutation(key, shards_of)[partner]
    strong = (owner == chosen) | (owner == (partner + shards_of // 2) % shards_of)
    return jnp.where(strong, factor * result, result)


def levels(key, dims, shards, smallest, high):
    gain, own = 1.0, jax.random.fold_in(key, 6)
    for position, blocks in shards:
        steps = jnp.exp(jax.random.uniform(jax.random.fold_in(own, position), (blocks,), jnp.float32, smallest / len(shards), high / len(shards)))
        gain = gain * jnp.repeat(steps, dims[position] // blocks).reshape([-1 if axis == position else 1 for axis in range(len(dims))])
    return gain


def split_up(amount, total, bound, skew):
    loads = [(1 << 20) // math.isqrt(standing ** skew) + 1 for standing in range(2, amount + 1)]
    rest, given = total - bound - (amount - 1), [1] * (amount - 1)
    while rest > 0:
        free = [i for i in range(amount - 1) if given[i] < bound]
        mass, left = sum([loads[i] for i in free]), rest
        for i in free:
            extra = min(bound - given[i], max(1, left * loads[i] // mass), rest)
            given[i] = given[i] + extra
            rest = rest - extra
    return np.array([bound] + given)


def uneven(stream_key, number_of, total, limit, slope):
    if number_of == 2:
        one = jax.random.randint(stream_key, (), max(1, total - limit), min(limit, total - 1) + 1)
        return jnp.stack([one, total - one])
    tallies = jnp.asarray(split_up(number_of, total, limit, slope), jnp.int32)
    twos = (number_of - 1) // 2
    source_of, taker = tallies[1:1 + 2 * twos:2], tallies[2:2 + 2 * twos:2]
    margin = jnp.minimum(source_of - 1, limit - taker)
    moved = jax.random.randint(jax.random.fold_in(stream_key, 1), (twos,), 0, 1 << 20) % (margin + 1)
    tallies = tallies.at[1:1 + 2 * twos:2].set(source_of - moved).at[2:2 + 2 * twos:2].set(taker + moved)
    return tallies[jax.random.permutation(jax.random.fold_in(stream_key, 2), number_of)]


def bell_draw(rng, extent, width, most, split=(), held_as=jnp.bfloat16):
    result = jax.random.normal(rng, extent, jnp.float32) * width
    if len(split) > 0:
        result = levels(rng, extent, split, -0.22, 0.18) * result
    return jnp.clip(result, min=-most, max=most).astype(held_as)


def heavy_noise(stream_key, shape, deviation, limit, shards, heavy, held_as=jnp.bfloat16):
    result = deviation * jax.random.normal(stream_key, shape, jnp.float32)
    if shards:
        result = result * levels(stream_key, shape, shards, -0.22, 0.18)
    return jnp.clip(raised(result, jax.random.fold_in(stream_key, 3), *heavy), -limit, limit).astype(held_as)


def setup_inputs(seed: int = 0) -> dict:
    key_of = jax.random.split(jax.random.key(seed), 11)
    return {
        "inputs": heavy_noise(key_of[0], (BATCH, LEN, C), 1.0, 12.0, ((0, 32), (1, 8)), (0, 2, 32, 2.75)),
        "doc_ids": jax.vmap(lambda own: jnp.searchsorted(jnp.cumsum(uneven(own, 4, LEN, LEN // 2, 0)), jnp.arange(LEN), side="right"))(jax.random.split(key_of[1], BATCH)).reshape((BATCH, LEN)).astype(jnp.int32),
        "dilation": jax.random.randint(key_of[2], (1,), 1, 2 * TD + 1).astype(jnp.int32),
        "filter_w": bell_draw(key_of[3], (2, C, C), (2 * C) ** -0.5, 0.09375, ((1, 32), (2, 8))),
        "gate_w": bell_draw(key_of[4], (2, C, C), (2 * C) ** -0.5, 0.09375, ((1, 32), (2, 8))),
        "filter_m": bell_draw(key_of[5], (2, C, C), 0.002, 0.01171875, ((1, 32), (2, 8)), jnp.float32),
        "filter_v": jnp.clip(jnp.exp(math.log(3.999999989900971e-06) - 3.6888794 * jax.random.uniform(key_of[6], (2, C, C), jnp.float32) ** levels(key_of[6], (2, C, C), ((1, 32), (2, 8)), -0.2, 0.2)), 1.0000000116860974e-07, 3.999999989900971e-06),
        "gate_m": bell_draw(key_of[7], (2, C, C), 0.002, 0.01171875, ((1, 32), (2, 8)), jnp.float32),
        "gate_v": jnp.clip(jnp.exp(math.log(3.999999989900971e-06) - 3.6888794 * jax.random.uniform(key_of[8], (2, C, C), jnp.float32) ** levels(key_of[8], (2, C, C), ((1, 32), (2, 8)), -0.2, 0.2)), 1.0000000116860974e-07, 3.999999989900971e-06),
        "cotangent": bell_draw(key_of[9], (BATCH, LEN, C), 1.0, 6.0, ((0, 32), (1, 8))),
    }


BETA_ONE = 0.9
BETA_TWO = 0.95
LEARN_RATE = 0.001
EPSILON = 1e-08

def lagged_rows(sequence, seq_ids, shift_by):
    length = sequence.shape[0]
    start_row = (length - shift_by).astype(jnp.int32)
    padded = jnp.concatenate([jnp.zeros_like(sequence), sequence], axis=0)
    shifted = lax.dynamic_slice_in_dim(padded, start_row, length, 0)
    id_padded = jnp.concatenate([jnp.full((length,), -1, jnp.int32), seq_ids], axis=0)
    id_shifted = lax.dynamic_slice_in_dim(id_padded, start_row, length, 0)
    return jnp.where((id_shifted == seq_ids)[:, None], shifted, jnp.zeros_like(shifted))

def leading_rows(values, seq_ids, shift_by):
    length = values.shape[0]
    start_row = shift_by.astype(jnp.int32)
    padded = jnp.concatenate([values, jnp.zeros_like(values)], axis=0)
    rows_ahead = lax.dynamic_slice_in_dim(padded, start_row, length, 0)
    id_padded = jnp.concatenate([seq_ids, jnp.full((length,), -1, jnp.int32)], axis=0)
    ids_ahead = lax.dynamic_slice_in_dim(id_padded, start_row, length, 0)
    return jnp.where((ids_ahead == seq_ids)[:, None], rows_ahead, jnp.zeros_like(rows_ahead))

def adam_update(weight, moment, second, gradient):
    new_moment = BETA_ONE * moment + (1.0 - BETA_ONE) * gradient
    new_second = BETA_TWO * second + (1.0 - BETA_TWO) * gradient * gradient
    first_fix = 1.0 - BETA_ONE ** STEP
    second_fix = 1.0 - BETA_TWO ** STEP
    step_size = new_moment / first_fix / (jnp.sqrt(new_second / second_fix) + EPSILON)
    new_weight = (weight.astype(jnp.float32) - LEARN_RATE * step_size).astype(jnp.bfloat16)
    return (new_weight, new_moment, new_second)

def reference(inputs, doc_ids, dilation, filter_w, gate_w, filter_m, filter_v, gate_m, gate_v, cotangent):
    shift_by = dilation[0]
    tap_zero = jnp.concatenate([filter_w[0], gate_w[0]], axis=1)
    tap_one = jnp.concatenate([filter_w[1], gate_w[1]], axis=1)

    def one_sequence(totals, members):
        sequence, seq_ids, seq_cotangent = members
        lagged = lagged_rows(sequence, seq_ids, shift_by)
        pre_act = jnp.dot(sequence, tap_zero, preferred_element_type=jnp.float32) + jnp.dot(lagged, tap_one, preferred_element_type=jnp.float32)
        filter_tanh = jnp.tanh(pre_act[:, :C])
        gate_sigmoid = jax.nn.sigmoid(pre_act[:, C:])
        gated_vals = (filter_tanh * gate_sigmoid).astype(jnp.bfloat16)
        layer_rows = (sequence.astype(jnp.float32) + gated_vals.astype(jnp.float32)).astype(jnp.bfloat16)
        cot_float = seq_cotangent.astype(jnp.float32)
        filter_delta = (cot_float * gate_sigmoid * (1.0 - filter_tanh * filter_tanh)).astype(jnp.bfloat16)
        gate_delta = (cot_float * filter_tanh * gate_sigmoid * (1.0 - gate_sigmoid)).astype(jnp.bfloat16)
        pre_grad = jnp.concatenate([filter_delta, gate_delta], axis=1)
        back_near = lax.dot_general(pre_grad, tap_zero, (((1,), (1,)), ((), ())), preferred_element_type=jnp.float32)
        back_far = lax.dot_general(pre_grad, tap_one, (((1,), (1,)), ((), ())), preferred_element_type=jnp.float32)
        grad_rows = (cot_float + back_near + leading_rows(back_far, seq_ids, shift_by)).astype(jnp.bfloat16)
        grad_zero = totals[0] + lax.dot_general(sequence, pre_grad, (((0,), (0,)), ((), ())), preferred_element_type=jnp.float32)
        grad_one = totals[1] + lax.dot_general(lagged, pre_grad, (((0,), (0,)), ((), ())), preferred_element_type=jnp.float32)
        return ((grad_zero, grad_one), (layer_rows, grad_rows))
    start_totals = (jnp.zeros((C, 2 * C), jnp.float32), jnp.zeros((C, 2 * C), jnp.float32))
    (grad_zero, grad_one), (layer_out, input_grad) = lax.scan(one_sequence, start_totals, (inputs, doc_ids, cotangent))
    filter_grad = jnp.stack([grad_zero[:, :C], grad_one[:, :C]], axis=0) / TOKENS
    gate_grad = jnp.stack([grad_zero[:, C:], grad_one[:, C:]], axis=0) / TOKENS
    new_filter_w, new_filter_m, new_filter_v = adam_update(filter_w, filter_m, filter_v, filter_grad)
    new_gate_w, new_gate_m, new_gate_v = adam_update(gate_w, gate_m, gate_v, gate_grad)
    return (layer_out, input_grad, new_filter_w, new_gate_w, new_filter_m, new_filter_v, new_gate_m, new_gate_v)
```

```python
import jax
import jax.numpy as jnp
from jax import lax
from jax.experimental import pallas as pl
from jax.experimental.pallas import tpu as pltpu
from jax.sharding import Mesh
from jax.sharding import PartitionSpec as P

STEP = 10
BETA_ONE = 0.9
BETA_TWO = 0.95
LEARN_RATE = 0.001
EPSILON = 1e-08

NX, NZ, NY, NC = 4, 8, 4, 2
ROWS = 128
LEN = 1024
CH = 2048
COLS = 256
KB = 64
PAD = 256
CA = 512
CB = 4 * COLS - CA
F32 = jnp.float32
BF16 = jnp.bfloat16
NSEM = 320
MESH = pl.DeviceIdType.MESH


def turn(position, by, size):
    return lax.rem(position + (by + size), size)


def kernel(
    dil_ref, x_in, ids_in, fw_in, gw_in, cot_in,
    lay_out, dx_out, grad_out,
    xb, xt, wb, u0, u1, dl, dd, cotc, gcol, grow, cotv, idc, idr, idsrc,
    dw, ra, za, rb, rbx, dxb, sib, yr, ssem, rsem, lsem,
):
    x, z = lax.axis_index("x"), lax.axis_index("z")
    y, c = lax.axis_index("y"), lax.axis_index("c")
    me = y * 2 + c
    d = dil_ref[0]

    def at_x(k):
        return turn(x, k, NX)

    def at_z(k):
        return turn(z, k, NZ)

    def at_y(k):
        return turn(y, k, NY)

    oc = 1 - c
    number = {}
    sent = []

    def slot(key):
        return number.setdefault(key, len(number))

    def send(key, src, dst, dev):
        i = slot(key)
        copy = pltpu.make_async_remote_copy(
            src_ref=src, dst_ref=dst, send_sem=ssem.at[i], recv_sem=rsem.at[i],
            device_id=dev, device_id_type=MESH,
        )
        copy.start()
        sent.append(copy)

    def arrived(key, dst, dev):
        i = slot(key)
        pltpu.make_async_remote_copy(
            src_ref=dst, dst_ref=dst, send_sem=ssem.at[i], recv_sem=rsem.at[i],
            device_id=dev, device_id_type=MESH,
        ).wait_recv()

    local = []

    def bring(src, dst):
        copy = pltpu.make_async_copy(src, dst, lsem.at[len(local)])
        copy.start()
        local.append(copy)

    def rows_of(ref, block):
        return ref.at[pl.ds(pl.multiple_of(block * ROWS, ROWS), ROWS)]

    def cols_of(ref, block):
        return ref.at[:, pl.ds(pl.multiple_of(block * COLS, COLS), COLS)]

    for tap in range(2):
        bring(fw_in.at[tap], wb.at[x, z, :, pl.ds(tap * 512, COLS)])
        bring(gw_in.at[tap], wb.at[x, z, :, pl.ds(tap * 512 + COLS, COLS)])
    bring(x_in, rows_of(xb, me))
    bring(cot_in, cotv)
    idsrc[...] = jnp.broadcast_to(ids_in[...], (8, ROWS))

    barrier = pltpu.get_barrier_semaphore()
    ctx_peers = [
        {"y": at_y(k), "c": cc} for k in range(4) for cc in (c, oc) if (k, cc is c) != (0, True)
    ]
    peers = ctx_peers + [{"x": at_x(k)} for k in (1, 2, 3)] + [{"z": at_z(k)} for k in (1, -1)]
    for dev in peers:
        pl.semaphore_signal(barrier, inc=1, device_id=dev, device_id_type=MESH)
    pl.semaphore_wait(barrier, len(peers))
    for copy in local:
        copy.wait()

    def wa(xi, zi, lo=0, n=KB):
        return wb.at[xi, zi, pl.ds(lo, n), pl.ds(0, CA)]

    def wbp(xi, zi):
        return wb.at[xi, zi, :, pl.ds(CA, CB)]

    def half(block, h, ref=None):
        ref = xb if ref is None else ref
        return ref.at[pl.ds(pl.multiple_of(block * ROWS + h * 64, 64), 64)]

    ups = {"z": at_z(1)}
    downs = {"z": at_z(-1)}

    def z_send_a(r):
        if r < 3:
            send(("za", 1, r), wa(x, at_z(-r)), wa(x, at_z(-r)), ups)
            send(("za", -1, r), wa(x, at_z(r)), wa(x, at_z(r)), downs)
        else:
            send(("za", 1, r), wa(x, at_z(-r), 0, 32), wa(x, at_z(-r), 0, 32), ups)
            send(("za", -1, r), wa(x, at_z(r), 32, 32), wa(x, at_z(r), 32, 32), downs)

    def z_got_a(r):
        if r < 4:
            arrived(("za", 1, r - 1), wa(x, at_z(-r)), downs)
            arrived(("za", -1, r - 1), wa(x, at_z(r)), ups)
        else:
            arrived(("za", 1, r - 1), wa(x, at_z(-r), 0, 32), downs)
            arrived(("za", -1, r - 1), wa(x, at_z(r), 32, 32), ups)

    def x_send_a(r):
        for k in (1, 2, 3):
            send(("xa", r, k), wa(x, at_z(r)), wa(x, at_z(r)), {"x": at_x(k)})

    def x_got_a(r):
        for k in (1, 2, 3):
            arrived(("xa", r, k), wa(at_x(-k), at_z(r)), {"x": at_x(-k)})

    def carried(direction, r):
        return (0, 1, 2, 3) if r < 4 else ((0, 1) if direction > 0 else (2, 3))

    def z_send_b(r, k):
        for s, dev in ((1, ups), (-1, downs)):
            if k in carried(s, r + 1):
                ref = wbp(at_x(k), at_z(-s * r))
                send(("zb", s, r, k), ref, ref, dev)

    def z_got_b(r, k):
        for s, dev in ((1, downs), (-1, ups)):
            if k in carried(s, r):
                arrived(("zb", s, r - 1, k), wbp(at_x(k), at_z(-s * r)), dev)

    z_send_a(0)
    for k in (1, 2, 3):
        send(("xb", k), wbp(x, z), wbp(x, z), {"x": at_x(k)})
    for s, h in ((1, 0), (-1, 1)):
        send(("X", s, 0), half(me, h), half(me, h), {"y": at_y(s)})
    send(("Xc", 0), rows_of(xb, me), rows_of(xb, me), {"c": oc})
    z_send_b(0, 0)
    x_send_a(0)
    for s, h in ((1, 1), (-1, 0)):
        send(("X", s, 1), half(me, h), half(me, h), {"y": at_y(s)})
    ctx_offsets = [(k, o) for k in range(4) for o in (0, 1) if (k, o) != (0, 0)]

    def ctx_dev(k, o):
        return {"y": at_y(k), "c": turn(c, o, NC)}

    def ctx_id(k, o):
        return at_y(k) * 2 + turn(c, o, NC)

    for k, o in ctx_offsets:
        send(("id", k, o), idsrc, idr.at[me], ctx_dev(k, o))

    idr[me] = idsrc[...]
    idc[pl.ds(0, PAD)] = jnp.full((PAD, 128), -1, jnp.int32)
    idc[pl.ds(PAD + LEN, PAD)] = jnp.full((PAD, 128), -2, jnp.int32)
    u1[:, pl.ds(0, PAD)] = jnp.zeros((4, PAD, 128), F32)
    dl[:, pl.ds(LEN, PAD)] = jnp.zeros((4, PAD, 128), F32)

    def transposed(block):
        rows = pl.ds(pl.multiple_of(block * ROWS, ROWS), ROWS)

        @pl.loop(0, NX)
        def _(xi):
            part = xb[rows, pl.ds(pl.multiple_of(xi * 512, 512), 512)]
            xt[xi, :, :, rows] = part.T.reshape(NZ, KB, ROWS)

    z_got_a(1)
    z_send_a(1)
    for r in (1, -1):
        x_send_a(r)
    for k in (1, 2, 3):
        arrived(("xb", k), wbp(at_x(-k), z), {"x": at_x(-k)})
        z_send_b(0, 4 - k)
    z_got_b(1, 0)
    z_send_b(1, 0)
    transposed(me)
    arrived(("X", 1, 0), half(at_y(-1) * 2 + c, 0), {"y": at_y(-1)})
    send(("X", 1, 2), half(at_y(-1) * 2 + c, 0), half(at_y(-1) * 2 + c, 0), {"y": at_y(1)})
    arrived(("X", -1, 0), half(at_y(1) * 2 + c, 1), {"y": at_y(1)})
    send(("X", -1, 2), half(at_y(1) * 2 + c, 1), half(at_y(1) * 2 + c, 1), {"y": at_y(-1)})
    z_got_a(2)
    z_send_a(2)
    for r in (2, -2):
        x_send_a(r)
    for k, o in ctx_offsets:
        send(("cot", k, o), cols_of(cotv, ctx_id(k, o)), rows_of(cotc, me), ctx_dev(k, o))
    for part in range(2):
        rows = pl.ds(pl.multiple_of(me * ROWS + part * 64, 64), 64)
        cotc[rows] = cotv[pl.ds(part * 64, 64), pl.ds(pl.multiple_of(me * COLS, COLS), COLS)]
    arrived(("Xc", 0), rows_of(xb, y * 2 + oc), {"c": oc})
    transposed(y * 2 + oc)
    for k in (3, 2, 1):
        z_got_b(1, k)
        z_send_b(1, k)
    arrived(("X", 1, 1), half(at_y(-1) * 2 + c, 1), {"y": at_y(-1)})
    send(("Xc", 1), rows_of(xb, at_y(-1) * 2 + c), rows_of(xb, at_y(-1) * 2 + c), {"c": oc})
    arrived(("X", -1, 1), half(at_y(1) * 2 + c, 0), {"y": at_y(1)})
    send(("Xc", 2), rows_of(xb, at_y(1) * 2 + c), rows_of(xb, at_y(1) * 2 + c), {"c": oc})
    z_got_a(3)
    z_send_a(3)
    for r in (3, -3):
        x_send_a(r)
    z_got_b(2, 0)
    z_send_b(2, 0)
    transposed(at_y(-1) * 2 + c)
    z_got_b(2, 3)
    z_send_b(2, 3)
    transposed(at_y(1) * 2 + c)
    for k in (2, 1):
        z_got_b(2, k)
        z_send_b(2, k)
    z_got_a(4)
    x_send_a(4)
    arrived(("Xc", 1), rows_of(xb, at_y(-1) * 2 + oc), {"c": oc})
    transposed(at_y(-1) * 2 + oc)
    arrived(("Xc", 2), rows_of(xb, at_y(1) * 2 + oc), {"c": oc})
    transposed(at_y(1) * 2 + oc)
    z_got_b(3, 0)
    z_send_b(3, 0)
    z_got_b(3, 3)
    z_send_b(3, 3)
    arrived(("X", 1, 2), half(at_y(2) * 2 + c, 0), {"y": at_y(-1)})
    arrived(("X", -1, 2), half(at_y(2) * 2 + c, 1), {"y": at_y(1)})
    send(("Xc", 3), rows_of(xb, at_y(2) * 2 + c), rows_of(xb, at_y(2) * 2 + c), {"c": oc})
    for k in (2, 1):
        z_got_b(3, k)
        z_send_b(3, k)
    transposed(at_y(2) * 2 + c)
    for k, o in ctx_offsets:
        arrived(("id", k, o), idr.at[ctx_id(-k, o)], ctx_dev(-k, o))

    @pl.loop(0, NY * NC)
    def _(block):
        spread = jnp.broadcast_to(idr[block, 0:1, :], (ROWS, ROWS))
        idc[pl.ds(pl.multiple_of(PAD + block * ROWS, ROWS), ROWS)] = spread.T

    arrived(("Xc", 3), rows_of(xb, at_y(2) * 2 + oc), {"c": oc})
    transposed(at_y(2) * 2 + oc)

    def forward(pair, first):
        @pl.loop(0, 4)
        def _(i):
            rows = pl.ds(pl.multiple_of(i * 256, 256), 256)
            lags = pl.ds(pl.multiple_of(PAD + i * 256, 256), 256)
            lhs = jnp.concatenate(
                [
                    xb[rows, pl.ds(pl.multiple_of(xi * 512 + pair * 128, 128), 128)]
                    for xi in range(NX)
                ],
                axis=1,
            )
            w0 = wb[:, pl.ds(pair * 2, 2), :, pl.ds(0, 512)].reshape(512, 512)
            w1 = wb[:, pl.ds(pair * 2, 2), :, pl.ds(512, 512)].reshape(512, 512)
            p0 = jnp.dot(lhs, w0, preferred_element_type=F32)
            p1 = jnp.dot(lhs, w1, preferred_element_type=F32)
            u0[rows] = p0 if first else u0[rows] + p0
            for j in range(4):
                part = p1[:, j * 128 : j * 128 + 128]
                u1[j, lags] = part if first else u1[j, lags] + part

    pair = z // 2
    lean = 1 - 2 * lax.rem(z, 2)
    for r in (0, 1, -1):
        x_got_a(r)
    forward(pair, True)
    for r in (2, -2):
        x_got_a(r)
    forward(turn(pair, -lean, 4), False)
    for r in (3, -3):
        x_got_a(r)
    forward(turn(pair, lean, 4), False)
    x_got_a(4)
    for k in range(4):
        z_got_b(4, k)
    forward(turn(pair, 2, 4), False)
    for k, o in ctx_offsets:
        arrived(("cot", k, o), rows_of(cotc, ctx_id(-k, o)), ctx_dev(-k, o))

    @pl.loop(0, LEN // 128)
    def _(i):
        t0 = pl.multiple_of(i * 128, 128)
        same = idc[pl.ds(PAD + t0, 128)] == idc[pl.ds(PAD + t0 - d, 128)]
        for j in range(2):
            pre = []
            for part in range(2):
                cols = pl.ds(part * COLS + j * 128, 128)
                lag = u1[part * 2 + j, pl.ds(PAD + t0 - d, 128)]
                pre.append(u0[pl.ds(t0, 128), cols] + jnp.where(same, lag, 0.0))
            f = jnp.tanh(pre[0])
            g = jax.nn.sigmoid(pre[1])
            near = pl.ds(j * 128, 128)
            far = pl.ds(COLS + j * 128, 128)
            gcol[pl.ds(t0, 128), near] = (f * g).astype(BF16)
            cot = cotc[pl.ds(t0, 128), near].astype(F32)
            fd = (cot * g * (1.0 - f * f)).astype(BF16)
            gd = (cot * f * g * (1.0 - g)).astype(BF16)
            dd[pl.ds(t0, 128), near] = fd
            dd[pl.ds(t0, 128), far] = gd
            dl[j, pl.ds(t0, 128)] = fd.astype(F32)
            dl[2 + j, pl.ds(t0, 128)] = gd.astype(F32)

    for k, o in ctx_offsets:
        send(("gat", k, o), rows_of(gcol, ctx_id(k, o)), cols_of(grow, me), ctx_dev(k, o))
    for part in range(2):
        rows = pl.ds(pl.multiple_of(me * ROWS + part * 64, 64), 64)
        grow[pl.ds(part * 64, 64), pl.ds(pl.multiple_of(me * COLS, COLS), COLS)] = gcol[rows]

    @pl.loop(0, LEN // 128)
    def _(i):
        t0 = pl.multiple_of(i * 128, 128)
        same = idc[pl.ds(PAD + t0, 128)] == idc[pl.ds(PAD + t0 + d, 128)]
        for j in range(4):
            ahead = dl[j, pl.ds(t0 + d, 128)]
            dd[pl.ds(t0, 128), pl.ds(512 + j * 128, 128)] = jnp.where(same, ahead, 0.0).astype(BF16)

    def grad_w(r):
        zi = at_z(r)
        for part in range(2):
            lhs = xt[:, zi].reshape(NX * KB, LEN)
            out = jnp.dot(lhs, dd[:, pl.ds(part * 512, 512)], preferred_element_type=F32)
            dw[:, zi, :, pl.ds(part * 512, 512)] = out.astype(BF16).reshape(NX, KB, 512)

    def da(xi, zi, lo=0, n=KB):
        return dw.at[xi, zi, pl.ds(lo, n), pl.ds(0, CA)]

    def db(xi, zi):
        return dw.at[xi, zi, :, pl.ds(CA, CB)]

    def sum_x_send(r):
        for k in (1, 2, 3):
            send(("sxa", r, k), da(at_x(k), at_z(r)), ra.at[k - 1, at_z(r)], {"x": at_x(k)})

    def sum_x_got(r):
        for k in (1, 2, 3):
            arrived(("sxa", r, k), ra.at[k - 1, at_z(r)], {"x": at_x(-k)})

    def a_sum(r):
        zi = at_z(r)
        return (da(x, zi)[...].astype(F32) + ra[0, zi].astype(F32)) + (
            ra[1, zi].astype(F32) + ra[2, zi].astype(F32)
        )

    def a_far():
        sum_x_got(4)
        da(x, at_z(4))[...] = a_sum(4).astype(BF16)
        send(("sza", 1, 4), da(x, at_z(4), 0, 32), za.at[0, 3, pl.ds(0, 32)], ups)
        send(("sza", -1, 4), da(x, at_z(-4), 32, 32), za.at[1, 3, pl.ds(32, 32)], downs)

    def a_step(r):
        for s, h, dev, src in ((1, 0, ups, downs), (-1, 1, downs, ups)):
            sum_x_got(s * r)
            total = a_sum(s * r)
            ref = da(x, at_z(s * r))
            if r == 3:
                lo = pl.ds(h * 32, 32)
                arrived(("sza", s, r + 1), za.at[h, r, lo], src)
                ref[...] = total.astype(BF16)
                part = total[h * 32 : h * 32 + 32] + za[h, r, lo].astype(F32)
                da(x, at_z(s * r), h * 32, 32)[...] = part.astype(BF16)
            else:
                arrived(("sza", s, r + 1), za.at[h, r], src)
                ref[...] = (total + za[h, r].astype(F32)).astype(BF16)
            send(("sza", s, r), ref, za.at[h, r - 1], dev)

    def b_far():
        for s, h, dev in ((1, 0, ups), (-1, 1, downs)):
            for k in carried(s, 4):
                send(("szb", s, 4, k), db(at_x(k), at_z(s * 4)), rb.at[h, 3, k], dev)

    def b_step(r, k):
        for s, h, dev, src in ((1, 0, ups, downs), (-1, 1, downs, ups)):
            ref = db(at_x(k), at_z(s * r))
            if k in carried(s, r + 1):
                arrived(("szb", s, r + 1, k), rb.at[h, r, k], src)
                ref[...] = (ref[...].astype(F32) + rb[h, r, k].astype(F32)).astype(BF16)
            send(("szb", s, r, k), ref, rb.at[h, r - 1, k], dev)

    def b_last(k):
        for s, h, src in ((1, 0, downs), (-1, 1, ups)):
            arrived(("szb", s, 1, k), rb.at[h, 0, k], src)
        ref = db(at_x(k), z)
        total = ref[...].astype(F32) + (rb[0, 0, k].astype(F32) + rb[1, 0, k].astype(F32))
        if k == 0:
            grad_out[:, pl.ds(CA, CB)] = total
        else:
            ref[...] = total.astype(BF16)
            send(("sxb", k), ref, rbx.at[k - 1], {"x": at_x(k)})

    def grad_x(k):
        yi = at_y(k)
        lhs = dd[pl.ds(pl.multiple_of(yi * 256, 256), 256), :]

        @pl.loop(0, NX)
        def _(xi):
            out = lax.dot_general(
                lhs, wb[xi].reshape(512, 1024), (((1,), (1,)), ((), ())), preferred_element_type=F32
            )
            out = out.astype(BF16).reshape(NC, ROWS, 512)
            dxb[yi, :, :, pl.ds(pl.multiple_of(xi * 512, 512), 512)] = out

        send(("sib", k), dxb.at[yi, oc], sib.at[yi], {"c": oc})

    def pair_sum(k):
        yi = at_y(k)
        arrived(("sib", k), sib.at[yi], {"c": oc})

        @pl.loop(0, 4)
        def _(i):
            rows = pl.ds(pl.multiple_of(i * 32, 32), 32)
            total = dxb[yi, c, rows].astype(F32) + sib[yi, rows].astype(F32)
            dxb[yi, c, rows] = total.astype(BF16)

    def y_far():
        pair_sum(2)
        for s, h in ((1, 0), (-1, 1)):
            rows = pl.ds(h * 64, 64)
            send(("y", s, 2), dxb.at[at_y(2), c, rows], yr.at[h, 0, rows], {"y": at_y(s)})

    def y_step():
        for s, h in ((1, 0), (-1, 1)):
            pair_sum(s)
            rows = pl.ds(h * 64, 64)
            yi = at_y(s)
            arrived(("y", s, 2), yr.at[h, 0, rows], {"y": at_y(-s)})

            @pl.loop(0, 2)
            def _(i):
                some = pl.ds(pl.multiple_of(h * 64 + i * 32, 32), 32)
                total = dxb[yi, c, some].astype(F32) + yr[h, 0, some].astype(F32)
                dxb[yi, c, some] = total.astype(BF16)

            send(("y", s, 1), dxb.at[yi, c], yr.at[h, 1], {"y": at_y(s)})

    grad_w(4)
    sum_x_send(4)
    b_far()
    grad_x(2)
    grad_w(3)
    sum_x_send(3)
    grad_w(-3)
    sum_x_send(-3)
    y_far()
    for k in range(4):
        b_step(3, k)
    a_far()
    grad_x(1)
    grad_w(2)
    sum_x_send(2)
    grad_w(-2)
    sum_x_send(-2)
    grad_x(-1)
    for k in range(4):
        b_step(2, k)
    a_step(3)
    y_step()
    grad_w(1)
    sum_x_send(1)
    grad_w(-1)
    sum_x_send(-1)
    grad_w(0)
    sum_x_send(0)
    a_step(2)
    grad_x(0)
    for k in range(4):
        b_step(1, k)
    for k, o in ctx_offsets:
        arrived(("gat", k, o), cols_of(grow, ctx_id(-k, o)), ctx_dev(-k, o))

    @pl.loop(0, 4)
    def _(i):
        rows = pl.ds(pl.multiple_of(i * 32, 32), 32)
        mine = xb[pl.ds(pl.multiple_of(me * ROWS + i * 32, 32), 32)]
        lay_out[rows] = (mine.astype(F32) + grow[rows].astype(F32)).astype(BF16)

    pair_sum(0)
    a_step(1)
    for k in (1, 2, 3, 0):
        b_last(k)
    for s, h in ((1, 0), (-1, 1)):
        arrived(("y", s, 1), yr.at[h, 1], {"y": at_y(-s)})

    @pl.loop(0, 4)
    def _(i):
        rows = pl.ds(pl.multiple_of(i * 32, 32), 32)
        back = dxb[y, c, rows].astype(F32) + (yr[0, 1, rows].astype(F32) + yr[1, 1, rows].astype(F32))
        dx_out[rows] = (cotv[rows].astype(F32) + back).astype(BF16)

    sum_x_got(0)
    total = a_sum(0)
    for s, h, src in ((1, 0, downs), (-1, 1, ups)):
        arrived(("sza", s, 1), za.at[h, 0], src)
    grad_out[:, pl.ds(0, CA)] = total + (za[0, 0].astype(F32) + za[1, 0].astype(F32))
    for k in (1, 2, 3):
        arrived(("sxb", k), rbx.at[k - 1], {"x": at_x(-k)})
    grad_out[:, pl.ds(CA, CB)] += rbx[0].astype(F32) + rbx[1].astype(F32) + rbx[2].astype(F32)
    for copy in sent:
        copy.wait_send()


def fused(dilation, inputs, ids, fw, gw, cot):
    any_space = pl.BlockSpec(memory_space=pl.ANY)
    vmem = pl.BlockSpec(memory_space=pltpu.VMEM)
    scratch = [
        ((LEN, CH), BF16),
        ((NX, NZ, KB, LEN), BF16),
        ((NX, NZ, KB, 4 * COLS), BF16),
        ((LEN, 2 * COLS), F32),
        ((4, PAD + LEN, 128), F32),
        ((4, LEN + PAD, 128), F32),
        ((LEN, 4 * COLS), BF16),
        ((LEN, COLS), BF16),
        ((LEN, COLS), BF16),
        ((ROWS, CH), BF16),
        ((ROWS, CH), BF16),
        ((PAD + LEN + PAD, 128), jnp.int32),
        ((NY * NC, 8, ROWS), jnp.int32),
        ((8, ROWS), jnp.int32),
        ((NX, NZ, KB, 4 * COLS), BF16),
        ((3, NZ, KB, CA), BF16),
        ((2, 4, KB, CA), BF16),
        ((2, 4, NX, KB, CB), BF16),
        ((3, KB, CB), BF16),
        ((NY, NC, ROWS, CH), BF16),
        ((NY, ROWS, CH), BF16),
        ((2, 2, ROWS, CH), BF16),
    ]
    return pl.pallas_call(
        kernel,
        name="layer",
        out_shape=(
            jax.ShapeDtypeStruct((ROWS, CH), BF16),
            jax.ShapeDtypeStruct((ROWS, CH), BF16),
            jax.ShapeDtypeStruct((KB, 4 * COLS), F32),
        ),
        in_specs=[
            pl.BlockSpec(memory_space=pltpu.SMEM), any_space, vmem, any_space, any_space, any_space,
        ],
        out_specs=(vmem, vmem, vmem),
        scratch_shapes=[pltpu.VMEM(s, t) for s, t in scratch]
        + [
            pltpu.SemaphoreType.DMA((NSEM,)),
            pltpu.SemaphoreType.DMA((NSEM,)),
            pltpu.SemaphoreType.DMA((6,)),
        ],
        compiler_params=pltpu.CompilerParams(
            collective_id=0, has_side_effects=True, vmem_limit_bytes=60 * 2**20
        ),
        cost_estimate=pl.CostEstimate(flops=13 * 10**9, bytes_accessed=2**23, transcendentals=2**20),
    )(dilation, inputs, ids, fw, gw, cot)


def adam_update(weight, moment, second, gradient):
    new_moment = BETA_ONE * moment + (1.0 - BETA_ONE) * gradient
    new_second = BETA_TWO * second + (1.0 - BETA_TWO) * gradient * gradient
    first_fix = 1.0 - BETA_ONE**STEP
    second_fix = 1.0 - BETA_TWO**STEP
    step_size = new_moment / first_fix / (jnp.sqrt(new_second / second_fix) + EPSILON)
    new_weight = (weight.astype(F32) - LEARN_RATE * step_size).astype(BF16)
    return (new_weight, new_moment, new_second)


def per_device(inputs, doc_ids, dilation, fw, gw, fm, fv, gm, gv, cotangent):
    layer_out, input_grad, grads = fused(dilation, inputs[0], doc_ids, fw, gw, cotangent[0])
    grads = grads / (LEN * NX * NZ)
    filter_grad = jnp.stack([grads[:, 0:256], grads[:, 512:768]])
    gate_grad = jnp.stack([grads[:, 256:512], grads[:, 768:1024]])
    new_fw, new_fm, new_fv = adam_update(fw, fm, fv, filter_grad)
    new_gw, new_gm, new_gv = adam_update(gw, gm, gv, gate_grad)
    return (layer_out[None], input_grad[None], new_fw, new_gw, new_fm, new_fv, new_gm, new_gv)


def solution(mesh):
    torus = Mesh(mesh.devices.reshape(NX, NZ, NY, NC), ("x", "z", "y", "c"))
    dp, ctx = ("x", "z"), ("y", "c")
    rows, weights = P(dp, ctx, None), P(None, dp, ctx)
    return jax.shard_map(
        per_device,
        mesh=torus,
        in_specs=(rows, P(dp, ctx), P(), *[weights] * 6, rows),
        out_specs=(rows, rows, *[weights] * 6),
        check_vma=False,
    )
```

```python
import jax
import jax.numpy as jnp
from jax import lax
from jax.experimental import pallas as pl
from jax.experimental.pallas import tpu as pltpu
from jax.sharding import Mesh
from jax.sharding import PartitionSpec as P

STEP = 10
BETA_ONE = 0.9
BETA_TWO = 0.95
LEARN_RATE = 0.001
EPSILON = 1e-08

NX, NZ, NY, NC = 4, 8, 4, 2
ROWS = 128
LEN = 1024
CH = 2048
COLS = 256
KB = 64
PAD = 256
CA = 640
CB = 4 * COLS - CA
F32 = jnp.float32
BF16 = jnp.bfloat16
NSEM = 320
VMEM_LIMIT = 62 * 2**20
TR = 64
MESH = pl.DeviceIdType.MESH


def turn(position, by, size):
    return lax.rem(position + (by + size), size)


def kernel(
    dil_ref, x_in, ids_in, fw_in, gw_in, fm_in, fv_in, gm_in, gv_in, cot_in,
    lay_out, dx_out, fw_out, gw_out, fm_out, fv_out, gm_out, gv_out,
    xb, xt, wb, u0, u1, dl, dd, cotc, gcol, grow, cotv, idc, idr, idsrc,
    gsum, dw, ra, za, rb, rbx, dxb, sib, yr, fm, fv, gm, gv, ssem, rsem, lsem,
):
    x, z = lax.axis_index("x"), lax.axis_index("z")
    y, c = lax.axis_index("y"), lax.axis_index("c")
    me = y * 2 + c
    d = dil_ref[0]

    def at_x(k):
        return turn(x, k, NX)

    def at_z(k):
        return turn(z, k, NZ)

    def at_y(k):
        return turn(y, k, NY)

    oc = 1 - c
    number = {}
    sent = []

    def slot(key):
        return number.setdefault(key, len(number))

    def send(key, src, dst, dev):
        i = slot(key)
        copy = pltpu.make_async_remote_copy(
            src_ref=src, dst_ref=dst, send_sem=ssem.at[i], recv_sem=rsem.at[i],
            device_id=dev, device_id_type=MESH,
        )
        copy.start()
        sent.append(copy)

    def arrived(key, dst, dev):
        i = slot(key)
        pltpu.make_async_remote_copy(
            src_ref=dst, dst_ref=dst, send_sem=ssem.at[i], recv_sem=rsem.at[i],
            device_id=dev, device_id_type=MESH,
        ).wait_recv()

    local = []

    def bring(src, dst):
        copy = pltpu.make_async_copy(src, dst, lsem.at[len(local)])
        copy.start()
        local.append(copy)

    def rows_of(ref, block):
        return ref.at[pl.ds(pl.multiple_of(block * ROWS, ROWS), ROWS)]

    def cols_of(ref, block):
        return ref.at[:, pl.ds(pl.multiple_of(block * COLS, COLS), COLS)]

    for tap in range(2):
        bring(fw_in.at[tap], wb.at[x, z, :, pl.ds(tap * 512, COLS)])
        bring(gw_in.at[tap], wb.at[x, z, :, pl.ds(tap * 512 + COLS, COLS)])
    bring(x_in, rows_of(xb, me))
    bring(cot_in, cotv)
    for src, dst in ((fm_in, fm), (fv_in, fv), (gm_in, gm), (gv_in, gv)):
        bring(src, dst)
    states = local[6:]
    idsrc[...] = jnp.broadcast_to(ids_in[...], (8, ROWS))

    barrier = pltpu.get_barrier_semaphore()
    ctx_peers = [
        {"y": at_y(k), "c": cc} for k in range(4) for cc in (c, oc) if (k, cc is c) != (0, True)
    ]
    peers = ctx_peers + [{"x": at_x(k)} for k in (1, 2, 3)] + [{"z": at_z(k)} for k in (1, -1)]
    for dev in peers:
        pl.semaphore_signal(barrier, inc=1, device_id=dev, device_id_type=MESH)
    pl.semaphore_wait(barrier, len(peers))
    for copy in local[:6]:
        copy.wait()

    def wa(xi, zi, lo=0, n=KB):
        return wb.at[xi, zi, pl.ds(lo, n), pl.ds(0, CA)]

    def wbp(xi, zi):
        return wb.at[xi, zi, :, pl.ds(CA, CB)]

    def half(block, h, ref=None):
        ref = xb if ref is None else ref
        return ref.at[pl.ds(pl.multiple_of(block * ROWS + h * 64, 64), 64)]

    ups = {"z": at_z(1)}
    downs = {"z": at_z(-1)}

    def z_send_a(r):
        if r < 3:
            send(("za", 1, r), wa(x, at_z(-r)), wa(x, at_z(-r)), ups)
            send(("za", -1, r), wa(x, at_z(r)), wa(x, at_z(r)), downs)
        else:
            send(("za", 1, r), wa(x, at_z(-r), 0, 32), wa(x, at_z(-r), 0, 32), ups)
            send(("za", -1, r), wa(x, at_z(r), 32, 32), wa(x, at_z(r), 32, 32), downs)

    def z_got_a(r):
        if r < 4:
            arrived(("za", 1, r - 1), wa(x, at_z(-r)), downs)
            arrived(("za", -1, r - 1), wa(x, at_z(r)), ups)
        else:
            arrived(("za", 1, r - 1), wa(x, at_z(-r), 0, 32), downs)
            arrived(("za", -1, r - 1), wa(x, at_z(r), 32, 32), ups)

    def x_send_a(r):
        for k in (1, 2, 3) if r == 4 else (1, 3):
            send(("xa", r, k), wa(x, at_z(r)), wa(x, at_z(r)), {"x": at_x(k)})

    def x_relay_a(r):
        for k, lo in ((1, 0), (3, 32)):
            arrived(("xa", r, k), wa(at_x(-k), at_z(r)), {"x": at_x(-k)})
            ref = wa(at_x(-k), at_z(r), lo, 32)
            send(("xr", r, k), ref, ref, {"x": at_x(k)})

    def x_got_a(r):
        if r == 4:
            for k in (1, 2, 3):
                arrived(("xa", r, k), wa(at_x(-k), at_z(r)), {"x": at_x(-k)})
        else:
            for k, lo in ((1, 0), (3, 32)):
                arrived(("xr", r, k), wa(at_x(2), at_z(r), lo, 32), {"x": at_x(-k)})

    def carried(direction, r):
        return (0, 1, 2, 3) if r < 4 else ((0, 1) if direction > 0 else (2, 3))

    def z_send_b(r, k):
        for s, dev in ((1, ups), (-1, downs)):
            if k in carried(s, r + 1):
                ref = wbp(at_x(k), at_z(-s * r))
                send(("zb", s, r, k), ref, ref, dev)

    def z_got_b(r, k):
        for s, dev in ((1, downs), (-1, ups)):
            if k in carried(s, r):
                arrived(("zb", s, r - 1, k), wbp(at_x(k), at_z(-s * r)), dev)

    z_send_a(0)
    for k in (1, 2, 3):
        send(("xb", k), wbp(x, z), wbp(x, z), {"x": at_x(k)})
    for s, h in ((1, 0), (-1, 1)):
        send(("X", s, 0), half(me, h), half(me, h), {"y": at_y(s)})
    send(("Xc", 0), rows_of(xb, me), rows_of(xb, me), {"c": oc})
    z_send_b(0, 0)
    x_send_a(0)
    for s, h in ((1, 1), (-1, 0)):
        send(("X", s, 1), half(me, h), half(me, h), {"y": at_y(s)})
    ctx_offsets = [(k, o) for k in range(4) for o in (0, 1) if (k, o) != (0, 0)]

    def ctx_dev(k, o):
        return {"y": at_y(k), "c": turn(c, o, NC)}

    def ctx_id(k, o):
        return at_y(k) * 2 + turn(c, o, NC)

    for k, o in ctx_offsets:
        send(("id", k, o), idsrc, idr.at[me], ctx_dev(k, o))

    idr[me] = idsrc[...]
    idc[pl.ds(0, PAD)] = jnp.full((PAD, 128), -1, jnp.int32)
    idc[pl.ds(PAD + LEN, PAD)] = jnp.full((PAD, 128), -2, jnp.int32)
    u1[:, pl.ds(0, PAD)] = jnp.zeros((4, PAD, 128), F32)
    dl[:, pl.ds(LEN, PAD)] = jnp.zeros((4, PAD, 128), F32)

    def transposed(block):
        rows = pl.ds(pl.multiple_of(block * ROWS, ROWS), ROWS)

        @pl.loop(0, NX)
        def _(xi):
            part = xb[rows, pl.ds(pl.multiple_of(xi * 512, 512), 512)]
            xt[xi, :, :, rows] = part.T.reshape(NZ, KB, ROWS)

    z_got_a(1)
    z_send_a(1)
    for r in (1, -1):
        x_send_a(r)
    for k in (1, 2, 3):
        arrived(("xb", k), wbp(at_x(-k), z), {"x": at_x(-k)})
        z_send_b(0, 4 - k)
    z_got_b(1, 0)
    z_send_b(1, 0)
    x_relay_a(0)
    transposed(me)
    arrived(("X", 1, 0), half(at_y(-1) * 2 + c, 0), {"y": at_y(-1)})
    send(("X", 1, 2), half(at_y(-1) * 2 + c, 0), half(at_y(-1) * 2 + c, 0), {"y": at_y(1)})
    arrived(("X", -1, 0), half(at_y(1) * 2 + c, 1), {"y": at_y(1)})
    send(("X", -1, 2), half(at_y(1) * 2 + c, 1), half(at_y(1) * 2 + c, 1), {"y": at_y(-1)})
    z_got_a(2)
    z_send_a(2)
    for r in (2, -2):
        x_send_a(r)
    for k, o in ctx_offsets:
        send(("cot", k, o), cols_of(cotv, ctx_id(k, o)), rows_of(cotc, me), ctx_dev(k, o))
    for part in range(2):
        rows = pl.ds(pl.multiple_of(me * ROWS + part * 64, 64), 64)
        cotc[rows] = cotv[pl.ds(part * 64, 64), pl.ds(pl.multiple_of(me * COLS, COLS), COLS)]
    arrived(("Xc", 0), rows_of(xb, y * 2 + oc), {"c": oc})
    transposed(y * 2 + oc)
    for k in (3, 2, 1):
        z_got_b(1, k)
        z_send_b(1, k)
    for r in (1, -1):
        x_relay_a(r)
    arrived(("X", 1, 1), half(at_y(-1) * 2 + c, 1), {"y": at_y(-1)})
    send(("Xc", 1), rows_of(xb, at_y(-1) * 2 + c), rows_of(xb, at_y(-1) * 2 + c), {"c": oc})
    arrived(("X", -1, 1), half(at_y(1) * 2 + c, 0), {"y": at_y(1)})
    send(("Xc", 2), rows_of(xb, at_y(1) * 2 + c), rows_of(xb, at_y(1) * 2 + c), {"c": oc})
    z_got_a(3)
    z_send_a(3)
    for r in (3, -3):
        x_send_a(r)
    z_got_b(2, 0)
    z_send_b(2, 0)
    transposed(at_y(-1) * 2 + c)
    z_got_b(2, 3)
    z_send_b(2, 3)
    transposed(at_y(1) * 2 + c)
    for k in (2, 1):
        z_got_b(2, k)
        z_send_b(2, k)
    for r in (2, -2):
        x_relay_a(r)
    z_got_a(4)
    x_send_a(4)
    arrived(("Xc", 1), rows_of(xb, at_y(-1) * 2 + oc), {"c": oc})
    transposed(at_y(-1) * 2 + oc)
    arrived(("Xc", 2), rows_of(xb, at_y(1) * 2 + oc), {"c": oc})
    transposed(at_y(1) * 2 + oc)
    z_got_b(3, 0)
    z_send_b(3, 0)
    z_got_b(3, 3)
    z_send_b(3, 3)
    arrived(("X", 1, 2), half(at_y(2) * 2 + c, 0), {"y": at_y(-1)})
    arrived(("X", -1, 2), half(at_y(2) * 2 + c, 1), {"y": at_y(1)})
    send(("Xc", 3), rows_of(xb, at_y(2) * 2 + c), rows_of(xb, at_y(2) * 2 + c), {"c": oc})
    for k in (2, 1):
        z_got_b(3, k)
        z_send_b(3, k)
    for r in (3, -3):
        x_relay_a(r)
    transposed(at_y(2) * 2 + c)
    for k, o in ctx_offsets:
        arrived(("id", k, o), idr.at[ctx_id(-k, o)], ctx_dev(-k, o))

    @pl.loop(0, NY * NC)
    def _(block):
        spread = jnp.broadcast_to(idr[block, 0:1, :], (ROWS, ROWS))
        idc[pl.ds(pl.multiple_of(PAD + block * ROWS, ROWS), ROWS)] = spread.T

    arrived(("Xc", 3), rows_of(xb, at_y(2) * 2 + oc), {"c": oc})
    transposed(at_y(2) * 2 + oc)

    def forward(pair, first):
        @pl.loop(0, 4)
        def _(i):
            rows = pl.ds(pl.multiple_of(i * 256, 256), 256)
            lags = pl.ds(pl.multiple_of(PAD + i * 256, 256), 256)
            lhs = jnp.concatenate(
                [
                    xb[rows, pl.ds(pl.multiple_of(xi * 512 + pair * 128, 128), 128)]
                    for xi in range(NX)
                ],
                axis=1,
            )
            w0 = wb[:, pl.ds(pair * 2, 2), :, pl.ds(0, 512)].reshape(512, 512)
            w1 = wb[:, pl.ds(pair * 2, 2), :, pl.ds(512, 512)].reshape(512, 512)
            p0 = jnp.dot(lhs, w0, preferred_element_type=F32)
            p1 = jnp.dot(lhs, w1, preferred_element_type=F32)
            u0[rows] = p0 if first else u0[rows] + p0
            for j in range(4):
                part = p1[:, j * 128 : j * 128 + 128]
                u1[j, lags] = part if first else u1[j, lags] + part

    pair = z // 2
    lean = 1 - 2 * lax.rem(z, 2)
    for r in (0, 1, -1):
        x_got_a(r)
    forward(pair, True)
    for r in (2, -2):
        x_got_a(r)
    forward(turn(pair, -lean, 4), False)
    for r in (3, -3):
        x_got_a(r)
    forward(turn(pair, lean, 4), False)
    x_got_a(4)
    for k in range(4):
        z_got_b(4, k)
    forward(turn(pair, 2, 4), False)
    for k, o in ctx_offsets:
        arrived(("cot", k, o), rows_of(cotc, ctx_id(-k, o)), ctx_dev(-k, o))

    @pl.loop(0, LEN // TR)
    def _(i):
        t0 = pl.multiple_of(i * TR, TR)
        same = idc[pl.ds(PAD + t0, TR)] == idc[pl.ds(PAD + t0 - d, TR)]
        for j in range(2):
            pre = []
            for part in range(2):
                cols = pl.ds(part * COLS + j * 128, 128)
                lag = u1[part * 2 + j, pl.ds(PAD + t0 - d, TR)]
                pre.append(u0[pl.ds(t0, TR), cols] + jnp.where(same, lag, 0.0))
            f = jnp.tanh(pre[0])
            g = 0.5 * jnp.tanh(0.5 * pre[1]) + 0.5
            near = pl.ds(j * 128, 128)
            far = pl.ds(COLS + j * 128, 128)
            gcol[pl.ds(t0, TR), near] = (f * g).astype(BF16)
            cot = cotc[pl.ds(t0, TR), near].astype(F32) * g
            fd = (cot * (1.0 - f * f)).astype(BF16)
            gd = (cot * f * (1.0 - g)).astype(BF16)
            dd[pl.ds(t0, TR), near] = fd
            dd[pl.ds(t0, TR), far] = gd
            dl[j, pl.ds(t0, TR)] = fd.astype(F32)
            dl[2 + j, pl.ds(t0, TR)] = gd.astype(F32)

    for k, o in ctx_offsets:
        send(("gat", k, o), rows_of(gcol, ctx_id(k, o)), cols_of(grow, me), ctx_dev(k, o))
    for part in range(2):
        rows = pl.ds(pl.multiple_of(me * ROWS + part * 64, 64), 64)
        grow[pl.ds(part * 64, 64), pl.ds(pl.multiple_of(me * COLS, COLS), COLS)] = gcol[rows]

    @pl.loop(0, LEN // TR)
    def _(i):
        t0 = pl.multiple_of(i * TR, TR)
        same = idc[pl.ds(PAD + t0, TR)] == idc[pl.ds(PAD + t0 + d, TR)]
        for j in range(4):
            ahead = dl[j, pl.ds(t0 + d, TR)]
            dd[pl.ds(t0, TR), pl.ds(512 + j * 128, 128)] = jnp.where(same, ahead, 0.0).astype(BF16)

    def grad_w(r):
        zi = at_z(r)
        for part in range(2):
            lhs = xt[:, zi].reshape(NX * KB, LEN)
            out = jnp.dot(lhs, dd[:, pl.ds(part * 512, 512)], preferred_element_type=F32)
            dw[:, zi, :, pl.ds(part * 512, 512)] = out.astype(BF16).reshape(NX, KB, 512)

    def da(xi, zi, lo=0, n=KB):
        return dw.at[xi, zi, pl.ds(lo, n), pl.ds(0, CA)]

    def db(xi, zi):
        return dw.at[xi, zi, :, pl.ds(CA, CB)]

    def direct(r):
        return r in (4, 0)

    def sum_x_send(r):
        zi = at_z(r)
        if direct(r):
            for k in (1, 2, 3):
                send(("sxa", r, k), da(at_x(k), zi), ra.at[k - 1, zi], {"x": at_x(k)})
        else:
            for k, lo in ((1, 0), (3, 32)):
                dst = ra.at[1, zi, pl.ds(lo, 32)]
                send(("sxr", r, k), da(at_x(2), zi, lo, 32), dst, {"x": at_x(k)})

    def sum_x_relay(r):
        zi = at_z(r)
        for k, lo in ((1, 0), (3, 32)):
            rows = pl.ds(lo, 32)
            arrived(("sxr", r, k), ra.at[1, zi, rows], {"x": at_x(-k)})
            ref = da(at_x(k), zi, lo, 32)
            ref[...] = (ref[...].astype(F32) + ra[1, zi, rows].astype(F32)).astype(BF16)
            send(("sxa", r, k), da(at_x(k), zi), ra.at[k - 1, zi], {"x": at_x(k)})

    def sum_x_got(r):
        for k in (1, 2, 3) if direct(r) else (1, 3):
            arrived(("sxa", r, k), ra.at[k - 1, at_z(r)], {"x": at_x(-k)})

    def a_sum(r):
        zi = at_z(r)
        total = da(x, zi)[...].astype(F32) + ra[0, zi].astype(F32) + ra[2, zi].astype(F32)
        return total + ra[1, zi].astype(F32) if direct(r) else total

    def a_far():
        sum_x_got(4)
        da(x, at_z(4))[...] = a_sum(4).astype(BF16)
        send(("sza", 1, 4), da(x, at_z(4), 0, 32), za.at[0, 3, pl.ds(0, 32)], ups)
        send(("sza", -1, 4), da(x, at_z(-4), 32, 32), za.at[1, 3, pl.ds(32, 32)], downs)

    def a_step(r):
        for s, h, dev, src in ((1, 0, ups, downs), (-1, 1, downs, ups)):
            sum_x_got(s * r)
            total = a_sum(s * r)
            ref = da(x, at_z(s * r))
            if r == 3:
                lo = pl.ds(h * 32, 32)
                arrived(("sza", s, r + 1), za.at[h, r, lo], src)
                ref[...] = total.astype(BF16)
                part = total[h * 32 : h * 32 + 32] + za[h, r, lo].astype(F32)
                da(x, at_z(s * r), h * 32, 32)[...] = part.astype(BF16)
            else:
                arrived(("sza", s, r + 1), za.at[h, r], src)
                ref[...] = (total + za[h, r].astype(F32)).astype(BF16)
            send(("sza", s, r), ref, za.at[h, r - 1], dev)

    def b_far():
        for s, h, dev in ((1, 0, ups), (-1, 1, downs)):
            for k in carried(s, 4):
                send(("szb", s, 4, k), db(at_x(k), at_z(s * 4)), rb.at[h, 3, k], dev)

    def b_step(r, k):
        for s, h, dev, src in ((1, 0, ups, downs), (-1, 1, downs, ups)):
            ref = db(at_x(k), at_z(s * r))
            if k in carried(s, r + 1):
                arrived(("szb", s, r + 1, k), rb.at[h, r, k], src)
                ref[...] = (ref[...].astype(F32) + rb[h, r, k].astype(F32)).astype(BF16)
            send(("szb", s, r, k), ref, rb.at[h, r - 1, k], dev)

    def b_last(k):
        for s, h, src in ((1, 0, downs), (-1, 1, ups)):
            arrived(("szb", s, 1, k), rb.at[h, 0, k], src)
        ref = db(at_x(k), z)
        total = ref[...].astype(F32) + (rb[0, 0, k].astype(F32) + rb[1, 0, k].astype(F32))
        if k == 0:
            gsum[:, pl.ds(CA, CB)] = total
        else:
            ref[...] = total.astype(BF16)
            send(("sxb", k), ref, rbx.at[k - 1], {"x": at_x(k)})

    def grad_x(k):
        yi = at_y(k)
        lhs = dd[pl.ds(pl.multiple_of(yi * 256, 256), 256), :]

        @pl.loop(0, NX)
        def _(xi):
            out = lax.dot_general(
                lhs, wb[xi].reshape(512, 1024), (((1,), (1,)), ((), ())), preferred_element_type=F32
            )
            out = out.astype(BF16).reshape(NC, ROWS, 512)
            dxb[yi, :, :, pl.ds(pl.multiple_of(xi * 512, 512), 512)] = out

        send(("sib", k), dxb.at[yi, oc], sib.at[yi], {"c": oc})

    def pair_sum(k):
        yi = at_y(k)
        arrived(("sib", k), sib.at[yi], {"c": oc})

        @pl.loop(0, 4)
        def _(i):
            rows = pl.ds(pl.multiple_of(i * 32, 32), 32)
            total = dxb[yi, c, rows].astype(F32) + sib[yi, rows].astype(F32)
            dxb[yi, c, rows] = total.astype(BF16)

    def y_far():
        pair_sum(2)
        for s, h in ((1, 0), (-1, 1)):
            rows = pl.ds(h * 64, 64)
            send(("y", s, 2), dxb.at[at_y(2), c, rows], yr.at[h, 0, rows], {"y": at_y(s)})

    def y_step():
        for s, h in ((1, 0), (-1, 1)):
            pair_sum(s)
            rows = pl.ds(h * 64, 64)
            yi = at_y(s)
            arrived(("y", s, 2), yr.at[h, 0, rows], {"y": at_y(-s)})

            @pl.loop(0, 2)
            def _(i):
                some = pl.ds(pl.multiple_of(h * 64 + i * 32, 32), 32)
                total = dxb[yi, c, some].astype(F32) + yr[h, 0, some].astype(F32)
                dxb[yi, c, some] = total.astype(BF16)

            send(("y", s, 1), dxb.at[yi, c], yr.at[h, 1], {"y": at_y(s)})

    def adam(j):
        tap, gate, cols = j // 4, (j // 2) % 2, pl.ds((j % 2) * 128, 128)
        moment, second = ((fm, fv), (gm, gv))[gate]
        outs = ((fw_out, fm_out, fv_out), (gw_out, gm_out, gv_out))[gate]
        results = adam_update(
            wb[x, z, :, pl.ds(j * 128, 128)],
            moment[tap, :, cols],
            second[tap, :, cols],
            gsum[:, pl.ds(j * 128, 128)] * (1.0 / (LEN * NX * NZ)),
        )
        for out, result in zip(outs, results):
            out[tap, :, cols] = result

    def y_last():
        pair_sum(0)
        for s, h in ((1, 0), (-1, 1)):
            arrived(("y", s, 1), yr.at[h, 1], {"y": at_y(-s)})

        @pl.loop(0, 4)
        def _(i):
            rows = pl.ds(pl.multiple_of(i * 32, 32), 32)
            far = yr[0, 1, rows].astype(F32) + yr[1, 1, rows].astype(F32)
            back = dxb[y, c, rows].astype(F32) + far
            dx_out[rows] = (cotv[rows].astype(F32) + back).astype(BF16)

    def a_last():
        sum_x_got(0)
        total = a_sum(0)
        for s, h, src in ((1, 0, downs), (-1, 1, ups)):
            arrived(("sza", s, 1), za.at[h, 0], src)
        gsum[:, pl.ds(0, CA)] = total + (za[0, 0].astype(F32) + za[1, 0].astype(F32))
        for j in range(CA // 128):
            adam(j)

    def b_end():
        for k in (1, 2, 3):
            arrived(("sxb", k), rbx.at[k - 1], {"x": at_x(-k)})
        across = rbx[0].astype(F32) + rbx[1].astype(F32) + rbx[2].astype(F32)
        gsum[:, pl.ds(CA, CB)] += across
        for j in range(CA // 128, 8):
            adam(j)

    grad_w(4)
    sum_x_send(4)
    b_far()
    grad_x(2)
    grad_w(3)
    sum_x_send(3)
    grad_w(-3)
    sum_x_send(-3)
    y_far()
    grad_w(2)
    sum_x_send(2)
    grad_w(-2)
    sum_x_send(-2)
    for k in range(4):
        b_step(3, k)
    a_far()
    for r in (3, -3):
        sum_x_relay(r)
    grad_x(1)
    grad_x(-1)
    for k in range(4):
        b_step(2, k)
    y_step()
    grad_w(1)
    sum_x_send(1)
    grad_w(-1)
    sum_x_send(-1)
    for r in (2, -2):
        sum_x_relay(r)
    a_step(3)
    for k in range(4):
        b_step(1, k)
    grad_w(0)
    for r in (1, -1):
        sum_x_relay(r)
    sum_x_send(0)
    grad_x(0)
    a_step(2)
    for k, o in ctx_offsets:
        arrived(("gat", k, o), cols_of(grow, ctx_id(-k, o)), ctx_dev(-k, o))

    @pl.loop(0, 4)
    def _(i):
        rows = pl.ds(pl.multiple_of(i * 32, 32), 32)
        mine = xb[pl.ds(pl.multiple_of(me * ROWS + i * 32, 32), 32)]
        lay_out[rows] = (mine.astype(F32) + grow[rows].astype(F32)).astype(BF16)

    for k in (1, 2, 3, 0):
        b_last(k)
    a_step(1)
    for copy in states:
        copy.wait()
    y_last()
    b_end()
    a_last()
    for copy in sent:
        copy.wait_send()


def fused(dilation, inputs, ids, fw, gw, fm, fv, gm, gv, cot):
    hbm = pl.BlockSpec(memory_space=pltpu.HBM)
    vmem = pl.BlockSpec(memory_space=pltpu.VMEM)
    scratch = [
        ((LEN, CH), BF16),
        ((NX, NZ, KB, LEN), BF16),
        ((NX, NZ, KB, 4 * COLS), BF16),
        ((LEN, 2 * COLS), F32),
        ((4, PAD + LEN, 128), F32),
        ((4, LEN + PAD, 128), F32),
        ((LEN, 4 * COLS), BF16),
        ((LEN, COLS), BF16),
        ((LEN, COLS), BF16),
        ((ROWS, CH), BF16),
        ((ROWS, CH), BF16),
        ((PAD + LEN + PAD, 128), jnp.int32),
        ((NY * NC, 8, ROWS), jnp.int32),
        ((8, ROWS), jnp.int32),
        ((KB, 4 * COLS), F32),
        ((NX, NZ, KB, 4 * COLS), BF16),
        ((3, NZ, KB, CA), BF16),
        ((2, 4, KB, CA), BF16),
        ((2, 4, NX, KB, CB), BF16),
        ((3, KB, CB), BF16),
        ((NY, NC, ROWS, CH), BF16),
        ((NY, ROWS, CH), BF16),
        ((2, 2, ROWS, CH), BF16),
        *[((2, KB, COLS), F32)] * 4,
    ]
    rows = jax.ShapeDtypeStruct((ROWS, CH), BF16)
    weight = jax.ShapeDtypeStruct((2, KB, COLS), BF16)
    state = jax.ShapeDtypeStruct((2, KB, COLS), F32)
    return pl.pallas_call(
        kernel,
        name="layer",
        out_shape=(rows, rows, weight, weight, *[state] * 4),
        in_specs=[pl.BlockSpec(memory_space=pltpu.SMEM), hbm, vmem, *[hbm] * 7],
        out_specs=(vmem,) * 8,
        scratch_shapes=[pltpu.VMEM(s, t) for s, t in scratch]
        + [
            pltpu.SemaphoreType.DMA((NSEM,)),
            pltpu.SemaphoreType.DMA((NSEM,)),
            pltpu.SemaphoreType.DMA((10,)),
        ],
        compiler_params=pltpu.CompilerParams(
            collective_id=0, has_side_effects=True, vmem_limit_bytes=VMEM_LIMIT
        ),
        cost_estimate=pl.CostEstimate(flops=13 * 10**9, bytes_accessed=2**23, transcendentals=2**20),
    )(dilation, inputs, ids, fw, gw, fm, fv, gm, gv, cot)


def hand_over(*refs):
    count = len(refs) // 2
    for src, dst in zip(refs[:count], refs[count:]):
        dst[...] = src[...]


def placed(arrays):
    return pl.pallas_call(
        hand_over,
        name="hand_over",
        out_shape=tuple(jax.ShapeDtypeStruct(a.shape, a.dtype) for a in arrays),
        in_specs=[pl.BlockSpec(memory_space=pltpu.VMEM)] * len(arrays),
        out_specs=(pl.BlockSpec(memory_space=pltpu.VMEM),) * len(arrays),
    )(*arrays)


def adam_update(weight, moment, second, gradient):
    new_moment = BETA_ONE * moment + (1.0 - BETA_ONE) * gradient
    new_second = BETA_TWO * second + (1.0 - BETA_TWO) * gradient * gradient
    first_fix = 1.0 - BETA_ONE**STEP
    second_fix = 1.0 - BETA_TWO**STEP
    step_size = new_moment / first_fix / (jnp.sqrt(new_second / second_fix) + EPSILON)
    new_weight = (weight.astype(F32) - LEARN_RATE * step_size).astype(BF16)
    return (new_weight, new_moment, new_second)


def per_device(inputs, doc_ids, dilation, fw, gw, fm, fv, gm, gv, cotangent):
    results = fused(dilation, inputs[0], doc_ids, fw, gw, fm, fv, gm, gv, cotangent[0])
    layer_out, input_grad, *states = placed(results)
    return (layer_out[None], input_grad[None], *states)


def solution(mesh):
    torus = Mesh(mesh.devices.reshape(NX, NZ, NY, NC), ("x", "z", "y", "c"))
    dp, ctx = ("x", "z"), ("y", "c")
    rows, weights = P(dp, ctx, None), P(None, dp, ctx)
    return jax.shard_map(
        per_device,
        mesh=torus,
        in_specs=(rows, P(dp, ctx), P(), *[weights] * 6, rows),
        out_specs=(rows, rows, *[weights] * 6),
        check_vma=False,
    )
```

```python
import jax
import jax.numpy as jnp
from jax import lax
from jax.experimental import pallas as pl
from jax.experimental.pallas import tpu as pltpu
from jax.sharding import Mesh
from jax.sharding import PartitionSpec as P

STEP = 10
BETA_ONE = 0.9
BETA_TWO = 0.95
LEARN_RATE = 0.001
EPSILON = 1e-08

NX, NZ, NY, NC = 4, 8, 4, 2
ROWS = 128
LEN = 1024
CH = 2048
COLS = 256
KB = 64
PAD = 256
CA = 640
CB = 4 * COLS - CA
F32 = jnp.float32
BF16 = jnp.bfloat16
NSEM = 320
VMEM_LIMIT = 62 * 2**20
TR = 64
MESH = pl.DeviceIdType.MESH


def turn(position, by, size):
    return lax.rem(position + (by + size), size)


def kernel(
    dil_ref, x_in, ids_in, fw_in, gw_in, fm_in, fv_in, gm_in, gv_in, cot_in,
    lay_out, dx_out, fw_out, gw_out, fm_out, fv_out, gm_out, gv_out,
    xb, xt, wb, u0, u1, dl, dd, cotc, gcol, grow, cotv, idc, idr, idsrc,
    gsum, dw, ra, za, rb, rbx, dxb, sib, yr, fm, fv, gm, gv, ssem, rsem, lsem,
):
    x, z = lax.axis_index("x"), lax.axis_index("z")
    y, c = lax.axis_index("y"), lax.axis_index("c")
    me = y * 2 + c
    d = dil_ref[0]

    def at_x(k):
        return turn(x, k, NX)

    def at_z(k):
        return turn(z, k, NZ)

    def at_y(k):
        return turn(y, k, NY)

    oc = 1 - c
    number = {}
    sent = []

    def slot(key):
        return number.setdefault(key, len(number))

    def send(key, src, dst, dev):
        i = slot(key)
        copy = pltpu.make_async_remote_copy(
            src_ref=src, dst_ref=dst, send_sem=ssem.at[i], recv_sem=rsem.at[i],
            device_id=dev, device_id_type=MESH,
        )
        copy.start()
        sent.append(copy)

    def arrived(key, dst, dev):
        i = slot(key)
        pltpu.make_async_remote_copy(
            src_ref=dst, dst_ref=dst, send_sem=ssem.at[i], recv_sem=rsem.at[i],
            device_id=dev, device_id_type=MESH,
        ).wait_recv()

    local = []

    def bring(src, dst):
        copy = pltpu.make_async_copy(src, dst, lsem.at[len(local)])
        copy.start()
        local.append(copy)

    def rows_of(ref, block):
        return ref.at[pl.ds(pl.multiple_of(block * ROWS, ROWS), ROWS)]

    def cols_of(ref, block):
        return ref.at[:, pl.ds(pl.multiple_of(block * COLS, COLS), COLS)]

    for tap in range(2):
        bring(fw_in.at[tap], wb.at[x, z, :, pl.ds(tap * 512, COLS)])
        bring(gw_in.at[tap], wb.at[x, z, :, pl.ds(tap * 512 + COLS, COLS)])
    bring(x_in, rows_of(xb, me))
    bring(cot_in, cotv)
    for src, dst in ((fm_in, fm), (fv_in, fv), (gm_in, gm), (gv_in, gv)):
        bring(src, dst)
    states = local[6:]
    idsrc[...] = jnp.broadcast_to(ids_in[...], (8, ROWS))

    barrier = pltpu.get_barrier_semaphore()
    ctx_peers = [
        {"y": at_y(k), "c": cc} for k in range(4) for cc in (c, oc) if (k, cc is c) != (0, True)
    ]
    peers = ctx_peers + [{"x": at_x(k)} for k in (1, 2, 3)] + [{"z": at_z(k)} for k in (1, -1)]
    for dev in peers:
        pl.semaphore_signal(barrier, inc=1, device_id=dev, device_id_type=MESH)
    pl.semaphore_wait(barrier, len(peers))
    for copy in local[:6]:
        copy.wait()

    def wa(xi, zi, lo=0, n=KB):
        return wb.at[xi, zi, pl.ds(lo, n), pl.ds(0, CA)]

    def wbp(xi, zi):
        return wb.at[xi, zi, :, pl.ds(CA, CB)]

    def half(block, h, ref=None):
        ref = xb if ref is None else ref
        return ref.at[pl.ds(pl.multiple_of(block * ROWS + h * 64, 64), 64)]

    ups = {"z": at_z(1)}
    downs = {"z": at_z(-1)}

    def z_send_a(r):
        if r < 3:
            send(("za", 1, r), wa(x, at_z(-r)), wa(x, at_z(-r)), ups)
            send(("za", -1, r), wa(x, at_z(r)), wa(x, at_z(r)), downs)
        else:
            send(("za", 1, r), wa(x, at_z(-r), 0, 32), wa(x, at_z(-r), 0, 32), ups)
            send(("za", -1, r), wa(x, at_z(r), 32, 32), wa(x, at_z(r), 32, 32), downs)

    def z_got_a(r):
        if r < 4:
            arrived(("za", 1, r - 1), wa(x, at_z(-r)), downs)
            arrived(("za", -1, r - 1), wa(x, at_z(r)), ups)
        else:
            arrived(("za", 1, r - 1), wa(x, at_z(-r), 0, 32), downs)
            arrived(("za", -1, r - 1), wa(x, at_z(r), 32, 32), ups)

    def x_send_a(r):
        for k in (1, 2, 3) if r == 4 else (1, 3):
            send(("xa", r, k), wa(x, at_z(r)), wa(x, at_z(r)), {"x": at_x(k)})

    def x_relay_a(r):
        for k, lo in ((1, 0), (3, 32)):
            arrived(("xa", r, k), wa(at_x(-k), at_z(r)), {"x": at_x(-k)})
            ref = wa(at_x(-k), at_z(r), lo, 32)
            send(("xr", r, k), ref, ref, {"x": at_x(k)})

    def x_got_a(r):
        if r == 4:
            for k in (1, 2, 3):
                arrived(("xa", r, k), wa(at_x(-k), at_z(r)), {"x": at_x(-k)})
        else:
            for k, lo in ((1, 0), (3, 32)):
                arrived(("xr", r, k), wa(at_x(2), at_z(r), lo, 32), {"x": at_x(-k)})

    def carried(direction, r):
        return (0, 1, 2, 3) if r < 4 else ((0, 1) if direction > 0 else (2, 3))

    def z_send_b(r, k):
        for s, dev in ((1, ups), (-1, downs)):
            if k in carried(s, r + 1):
                ref = wbp(at_x(k), at_z(-s * r))
                send(("zb", s, r, k), ref, ref, dev)

    def z_got_b(r, k):
        for s, dev in ((1, downs), (-1, ups)):
            if k in carried(s, r):
                arrived(("zb", s, r - 1, k), wbp(at_x(k), at_z(-s * r)), dev)

    z_send_a(0)
    for k in (1, 2, 3):
        send(("xb", k), wbp(x, z), wbp(x, z), {"x": at_x(k)})
    for s, h in ((1, 0), (-1, 1)):
        send(("X", s, 0), half(me, h), half(me, h), {"y": at_y(s)})
    send(("Xc", 0), rows_of(xb, me), rows_of(xb, me), {"c": oc})
    z_send_b(0, 0)
    x_send_a(0)
    for s, h in ((1, 1), (-1, 0)):
        send(("X", s, 1), half(me, h), half(me, h), {"y": at_y(s)})
    ctx_offsets = [(k, o) for k in range(4) for o in (0, 1) if (k, o) != (0, 0)]

    def ctx_dev(k, o):
        return {"y": at_y(k), "c": turn(c, o, NC)}

    def ctx_id(k, o):
        return at_y(k) * 2 + turn(c, o, NC)

    for k, o in ctx_offsets:
        send(("id", k, o), idsrc, idr.at[me], ctx_dev(k, o))

    idr[me] = idsrc[...]
    idc[pl.ds(0, PAD)] = jnp.full((PAD, 128), -1, jnp.int32)
    idc[pl.ds(PAD + LEN, PAD)] = jnp.full((PAD, 128), -2, jnp.int32)
    u1[:, pl.ds(0, PAD)] = jnp.zeros((4, PAD, 128), F32)
    dl[:, pl.ds(LEN, PAD)] = jnp.zeros((4, PAD, 128), F32)

    def transposed(block):
        rows = pl.ds(pl.multiple_of(block * ROWS, ROWS), ROWS)

        @pl.loop(0, NX)
        def _(xi):
            part = xb[rows, pl.ds(pl.multiple_of(xi * 512, 512), 512)]
            xt[xi, :, :, rows] = part.T.reshape(NZ, KB, ROWS)

    z_got_a(1)
    z_send_a(1)
    for r in (1, -1):
        x_send_a(r)
    for k in (1, 2, 3):
        arrived(("xb", k), wbp(at_x(-k), z), {"x": at_x(-k)})
        z_send_b(0, 4 - k)
    z_got_b(1, 0)
    z_send_b(1, 0)
    x_relay_a(0)
    transposed(me)
    arrived(("X", 1, 0), half(at_y(-1) * 2 + c, 0), {"y": at_y(-1)})
    send(("X", 1, 2), half(at_y(-1) * 2 + c, 0), half(at_y(-1) * 2 + c, 0), {"y": at_y(1)})
    arrived(("X", -1, 0), half(at_y(1) * 2 + c, 1), {"y": at_y(1)})
    send(("X", -1, 2), half(at_y(1) * 2 + c, 1), half(at_y(1) * 2 + c, 1), {"y": at_y(-1)})
    z_got_a(2)
    z_send_a(2)
    for r in (2, -2):
        x_send_a(r)
    for k, o in ctx_offsets:
        send(("cot", k, o), cols_of(cotv, ctx_id(k, o)), rows_of(cotc, me), ctx_dev(k, o))
    for part in range(2):
        rows = pl.ds(pl.multiple_of(me * ROWS + part * 64, 64), 64)
        cotc[rows] = cotv[pl.ds(part * 64, 64), pl.ds(pl.multiple_of(me * COLS, COLS), COLS)]
    arrived(("Xc", 0), rows_of(xb, y * 2 + oc), {"c": oc})
    transposed(y * 2 + oc)
    for r in (1, -1):
        x_relay_a(r)
    for k in (3, 2, 1):
        z_got_b(1, k)
        z_send_b(1, k)
    arrived(("X", 1, 1), half(at_y(-1) * 2 + c, 1), {"y": at_y(-1)})
    send(("Xc", 1), rows_of(xb, at_y(-1) * 2 + c), rows_of(xb, at_y(-1) * 2 + c), {"c": oc})
    arrived(("X", -1, 1), half(at_y(1) * 2 + c, 0), {"y": at_y(1)})
    send(("Xc", 2), rows_of(xb, at_y(1) * 2 + c), rows_of(xb, at_y(1) * 2 + c), {"c": oc})
    z_got_a(3)
    z_send_a(3)
    for r in (3, -3):
        x_send_a(r)
    z_got_b(2, 0)
    z_send_b(2, 0)
    transposed(at_y(-1) * 2 + c)
    z_got_b(2, 3)
    z_send_b(2, 3)
    for r in (2, -2):
        x_relay_a(r)
    transposed(at_y(1) * 2 + c)
    for k in (2, 1):
        z_got_b(2, k)
        z_send_b(2, k)
    z_got_a(4)
    x_send_a(4)
    arrived(("Xc", 1), rows_of(xb, at_y(-1) * 2 + oc), {"c": oc})
    transposed(at_y(-1) * 2 + oc)
    arrived(("Xc", 2), rows_of(xb, at_y(1) * 2 + oc), {"c": oc})
    transposed(at_y(1) * 2 + oc)
    z_got_b(3, 0)
    z_send_b(3, 0)
    z_got_b(3, 3)
    z_send_b(3, 3)
    for r in (3, -3):
        x_relay_a(r)
    arrived(("X", 1, 2), half(at_y(2) * 2 + c, 0), {"y": at_y(-1)})
    arrived(("X", -1, 2), half(at_y(2) * 2 + c, 1), {"y": at_y(1)})
    send(("Xc", 3), rows_of(xb, at_y(2) * 2 + c), rows_of(xb, at_y(2) * 2 + c), {"c": oc})
    for k in (2, 1):
        z_got_b(3, k)
        z_send_b(3, k)
    transposed(at_y(2) * 2 + c)
    for k, o in ctx_offsets:
        arrived(("id", k, o), idr.at[ctx_id(-k, o)], ctx_dev(-k, o))

    @pl.loop(0, NY * NC)
    def _(block):
        spread = jnp.broadcast_to(idr[block, 0:1, :], (ROWS, ROWS))
        idc[pl.ds(pl.multiple_of(PAD + block * ROWS, ROWS), ROWS)] = spread.T

    arrived(("Xc", 3), rows_of(xb, at_y(2) * 2 + oc), {"c": oc})
    transposed(at_y(2) * 2 + oc)

    def forward(pair, first):
        @pl.loop(0, 1)
        def _(i):
            rows = pl.ds(pl.multiple_of(i * 1024, 512), 1024)
            lags = pl.ds(pl.multiple_of(PAD + i * 1024, 256), 1024)
            lhs = jnp.concatenate(
                [
                    xb[rows, pl.ds(pl.multiple_of(xi * 512 + pair * 128, 128), 128)]
                    for xi in range(NX)
                ],
                axis=1,
            )
            w0 = wb[:, pl.ds(pair * 2, 2), :, pl.ds(0, 512)].reshape(512, 512)
            w1 = wb[:, pl.ds(pair * 2, 2), :, pl.ds(512, 512)].reshape(512, 512)
            p0 = jnp.dot(lhs, w0, preferred_element_type=F32)
            p1 = jnp.dot(lhs, w1, preferred_element_type=F32)
            u0[rows] = p0 if first else u0[rows] + p0
            for j in range(4):
                part = p1[:, j * 128 : j * 128 + 128]
                u1[j, lags] = part if first else u1[j, lags] + part

    pair = z // 2
    lean = 1 - 2 * lax.rem(z, 2)
    for r in (0, 1, -1):
        x_got_a(r)
    forward(pair, True)
    for r in (2, -2):
        x_got_a(r)
    forward(turn(pair, -lean, 4), False)
    for r in (3, -3):
        x_got_a(r)
    forward(turn(pair, lean, 4), False)
    x_got_a(4)
    for k in range(4):
        z_got_b(4, k)
    forward(turn(pair, 2, 4), False)
    for k, o in ctx_offsets:
        arrived(("cot", k, o), rows_of(cotc, ctx_id(-k, o)), ctx_dev(-k, o))

    @pl.loop(0, LEN // TR)
    def _(i):
        t0 = pl.multiple_of(i * TR, TR)
        same = idc[pl.ds(PAD + t0, TR)] == idc[pl.ds(PAD + t0 - d, TR)]
        for j in range(2):
            pre = []
            for part in range(2):
                cols = pl.ds(part * COLS + j * 128, 128)
                lag = u1[part * 2 + j, pl.ds(PAD + t0 - d, TR)]
                pre.append(u0[pl.ds(t0, TR), cols] + jnp.where(same, lag, 0.0))
            f = jnp.tanh(pre[0])
            g = 0.5 * jnp.tanh(0.5 * pre[1]) + 0.5
            near = pl.ds(j * 128, 128)
            far = pl.ds(COLS + j * 128, 128)
            gcol[pl.ds(t0, TR), near] = (f * g).astype(BF16)
            cot = cotc[pl.ds(t0, TR), near].astype(F32) * g
            fd = (cot * (1.0 - f * f)).astype(BF16)
            gd = (cot * f * (1.0 - g)).astype(BF16)
            dd[pl.ds(t0, TR), near] = fd
            dd[pl.ds(t0, TR), far] = gd
            dl[j, pl.ds(t0, TR)] = fd.astype(F32)
            dl[2 + j, pl.ds(t0, TR)] = gd.astype(F32)

    for k, o in ctx_offsets:
        send(("gat", k, o), rows_of(gcol, ctx_id(k, o)), cols_of(grow, me), ctx_dev(k, o))
    for part in range(2):
        rows = pl.ds(pl.multiple_of(me * ROWS + part * 64, 64), 64)
        grow[pl.ds(part * 64, 64), pl.ds(pl.multiple_of(me * COLS, COLS), COLS)] = gcol[rows]

    @pl.loop(0, LEN // TR)
    def _(i):
        t0 = pl.multiple_of(i * TR, TR)
        same = idc[pl.ds(PAD + t0, TR)] == idc[pl.ds(PAD + t0 + d, TR)]
        for j in range(4):
            ahead = dl[j, pl.ds(t0 + d, TR)]
            dd[pl.ds(t0, TR), pl.ds(512 + j * 128, 128)] = jnp.where(same, ahead, 0.0).astype(BF16)

    def grad_w(*steps):
        for part in range(2):
            cols = pl.ds(part * 512, 512)
            lhs = [xt[:, at_z(r)].reshape(NX * KB, LEN) for r in steps]
            out = jnp.dot(jnp.concatenate(lhs, axis=0), dd[:, cols], preferred_element_type=F32)
            for i, r in enumerate(steps):
                mine = out[i * 256 : i * 256 + 256].astype(BF16)
                dw[:, at_z(r), :, cols] = mine.reshape(NX, KB, 512)

    def da(xi, zi, lo=0, n=KB):
        return dw.at[xi, zi, pl.ds(lo, n), pl.ds(0, CA)]

    def db(xi, zi):
        return dw.at[xi, zi, :, pl.ds(CA, CB)]

    def direct(r):
        return r == 4

    def sum_x_send(r):
        zi = at_z(r)
        if direct(r):
            for k in (1, 2, 3):
                send(("sxa", r, k), da(at_x(k), zi), ra.at[k - 1, zi], {"x": at_x(k)})
        else:
            for k, lo in ((1, 0), (3, 32)):
                dst = ra.at[1, zi, pl.ds(lo, 32)]
                send(("sxr", r, k), da(at_x(2), zi, lo, 32), dst, {"x": at_x(k)})

    def sum_x_relay(r):
        zi = at_z(r)
        for k, lo in ((1, 0), (3, 32)):
            rows = pl.ds(lo, 32)
            arrived(("sxr", r, k), ra.at[1, zi, rows], {"x": at_x(-k)})
            ref = da(at_x(k), zi, lo, 32)
            ref[...] = (ref[...].astype(F32) + ra[1, zi, rows].astype(F32)).astype(BF16)
            send(("sxa", r, k), da(at_x(k), zi), ra.at[k - 1, zi], {"x": at_x(k)})

    def sum_x_got(r):
        for k in (1, 2, 3) if direct(r) else (1, 3):
            arrived(("sxa", r, k), ra.at[k - 1, at_z(r)], {"x": at_x(-k)})

    def a_sum(r):
        zi = at_z(r)
        total = da(x, zi)[...].astype(F32) + ra[0, zi].astype(F32) + ra[2, zi].astype(F32)
        return total + ra[1, zi].astype(F32) if direct(r) else total

    def a_far():
        sum_x_got(4)
        da(x, at_z(4))[...] = a_sum(4).astype(BF16)
        send(("sza", 1, 4), da(x, at_z(4), 0, 32), za.at[0, 3, pl.ds(0, 32)], ups)
        send(("sza", -1, 4), da(x, at_z(-4), 32, 32), za.at[1, 3, pl.ds(32, 32)], downs)

    def a_step(r):
        for s, h, dev, src in ((1, 0, ups, downs), (-1, 1, downs, ups)):
            sum_x_got(s * r)
            total = a_sum(s * r)
            ref = da(x, at_z(s * r))
            if r == 3:
                lo = pl.ds(h * 32, 32)
                arrived(("sza", s, r + 1), za.at[h, r, lo], src)
                ref[...] = total.astype(BF16)
                part = total[h * 32 : h * 32 + 32] + za[h, r, lo].astype(F32)
                da(x, at_z(s * r), h * 32, 32)[...] = part.astype(BF16)
            else:
                arrived(("sza", s, r + 1), za.at[h, r], src)
                ref[...] = (total + za[h, r].astype(F32)).astype(BF16)
            send(("sza", s, r), ref, za.at[h, r - 1], dev)

    def b_far():
        for s, h, dev in ((1, 0, ups), (-1, 1, downs)):
            for k in carried(s, 4):
                send(("szb", s, 4, k), db(at_x(k), at_z(s * 4)), rb.at[h, 3, k], dev)

    def b_step(r, k):
        for s, h, dev, src in ((1, 0, ups, downs), (-1, 1, downs, ups)):
            ref = db(at_x(k), at_z(s * r))
            if k in carried(s, r + 1):
                arrived(("szb", s, r + 1, k), rb.at[h, r, k], src)
                ref[...] = (ref[...].astype(F32) + rb[h, r, k].astype(F32)).astype(BF16)
            send(("szb", s, r, k), ref, rb.at[h, r - 1, k], dev)

    def b_last(k):
        for s, h, src in ((1, 0, downs), (-1, 1, ups)):
            arrived(("szb", s, 1, k), rb.at[h, 0, k], src)
        ref = db(at_x(k), z)
        total = ref[...].astype(F32) + (rb[0, 0, k].astype(F32) + rb[1, 0, k].astype(F32))
        if k == 0:
            gsum[:, pl.ds(CA, CB)] = total
        else:
            ref[...] = total.astype(BF16)
            send(("sxb", k), ref, rbx.at[k - 1], {"x": at_x(k)})

    def grad_x(k):
        yi = at_y(k)
        lhs = dd[pl.ds(pl.multiple_of(yi * 256, 256), 256), :]

        @pl.loop(0, NX)
        def _(xi):
            out = lax.dot_general(
                lhs, wb[xi].reshape(512, 1024), (((1,), (1,)), ((), ())), preferred_element_type=F32
            )
            out = out.astype(BF16).reshape(NC, ROWS, 512)
            dxb[yi, :, :, pl.ds(pl.multiple_of(xi * 512, 512), 512)] = out

        send(("sib", k), dxb.at[yi, oc], sib.at[yi], {"c": oc})

    def pair_sum(k):
        yi = at_y(k)
        arrived(("sib", k), sib.at[yi], {"c": oc})

        @pl.loop(0, 4)
        def _(i):
            rows = pl.ds(pl.multiple_of(i * 32, 32), 32)
            total = dxb[yi, c, rows].astype(F32) + sib[yi, rows].astype(F32)
            dxb[yi, c, rows] = total.astype(BF16)

    def y_far():
        pair_sum(2)
        for s, h in ((1, 0), (-1, 1)):
            rows = pl.ds(h * 64, 64)
            send(("y", s, 2), dxb.at[at_y(2), c, rows], yr.at[h, 0, rows], {"y": at_y(s)})

    def y_step():
        for s, h in ((1, 0), (-1, 1)):
            pair_sum(s)
            rows = pl.ds(h * 64, 64)
            yi = at_y(s)
            arrived(("y", s, 2), yr.at[h, 0, rows], {"y": at_y(-s)})

            @pl.loop(0, 2)
            def _(i):
                some = pl.ds(pl.multiple_of(h * 64 + i * 32, 32), 32)
                total = dxb[yi, c, some].astype(F32) + yr[h, 0, some].astype(F32)
                dxb[yi, c, some] = total.astype(BF16)

            send(("y", s, 1), dxb.at[yi, c], yr.at[h, 1], {"y": at_y(s)})

    def adam(j):
        tap, gate, cols = j // 4, (j // 2) % 2, pl.ds((j % 2) * 128, 128)
        moment, second = ((fm, fv), (gm, gv))[gate]
        outs = ((fw_out, fm_out, fv_out), (gw_out, gm_out, gv_out))[gate]
        results = adam_update(
            wb[x, z, :, pl.ds(j * 128, 128)],
            moment[tap, :, cols],
            second[tap, :, cols],
            gsum[:, pl.ds(j * 128, 128)] * (1.0 / (LEN * NX * NZ)),
        )
        for out, result in zip(outs, results):
            out[tap, :, cols] = result

    def y_last():
        pair_sum(0)
        for s, h in ((1, 0), (-1, 1)):
            arrived(("y", s, 1), yr.at[h, 1], {"y": at_y(-s)})

        @pl.loop(0, 4)
        def _(i):
            rows = pl.ds(pl.multiple_of(i * 32, 32), 32)
            far = yr[0, 1, rows].astype(F32) + yr[1, 1, rows].astype(F32)
            back = dxb[y, c, rows].astype(F32) + far
            dx_out[rows] = (cotv[rows].astype(F32) + back).astype(BF16)

    def a_last():
        sum_x_got(0)
        total = a_sum(0)
        for s, h, src in ((1, 0, downs), (-1, 1, ups)):
            arrived(("sza", s, 1), za.at[h, 0], src)
        gsum[:, pl.ds(0, CA)] = total + (za[0, 0].astype(F32) + za[1, 0].astype(F32))
        for j in range(CA // 128):
            adam(j)

    def b_end():
        for k in (1, 2, 3):
            arrived(("sxb", k), rbx.at[k - 1], {"x": at_x(-k)})
        across = rbx[0].astype(F32) + rbx[1].astype(F32) + rbx[2].astype(F32)
        gsum[:, pl.ds(CA, CB)] += across
        for j in range(CA // 128, 8):
            adam(j)

    grad_w(4)
    sum_x_send(4)
    b_far()
    grad_x(2)
    grad_w(3, -3)
    sum_x_send(3)
    sum_x_send(-3)
    grad_w(2)
    sum_x_send(2)
    for k in range(4):
        b_step(3, k)
    grad_w(-2)
    sum_x_send(-2)
    a_far()
    y_far()
    grad_x(1)
    for r in (3, -3):
        sum_x_relay(r)
    grad_w(1, -1)
    sum_x_send(1)
    sum_x_send(-1)
    for k in range(4):
        b_step(2, k)
    for r in (2, -2):
        sum_x_relay(r)
    grad_x(-1)
    grad_w(0)
    sum_x_send(0)
    a_step(3)
    y_step()
    for k in range(4):
        b_step(1, k)
    for r in (1, -1, 0):
        sum_x_relay(r)
    grad_x(0)
    a_step(2)
    for k, o in ctx_offsets:
        arrived(("gat", k, o), cols_of(grow, ctx_id(-k, o)), ctx_dev(-k, o))

    @pl.loop(0, 4)
    def _(i):
        rows = pl.ds(pl.multiple_of(i * 32, 32), 32)
        mine = xb[pl.ds(pl.multiple_of(me * ROWS + i * 32, 32), 32)]
        lay_out[rows] = (mine.astype(F32) + grow[rows].astype(F32)).astype(BF16)

    for k in (1, 2, 3, 0):
        b_last(k)
    a_step(1)
    for copy in states:
        copy.wait()
    y_last()
    b_end()
    a_last()
    for copy in sent:
        copy.wait_send()


def fused(dilation, inputs, ids, fw, gw, fm, fv, gm, gv, cot):
    hbm = pl.BlockSpec(memory_space=pltpu.HBM)
    vmem = pl.BlockSpec(memory_space=pltpu.VMEM)
    scratch = [
        ((LEN, CH), BF16),
        ((NX, NZ, KB, LEN), BF16),
        ((NX, NZ, KB, 4 * COLS), BF16),
        ((LEN, 2 * COLS), F32),
        ((4, PAD + LEN, 128), F32),
        ((4, LEN + PAD, 128), F32),
        ((LEN, 4 * COLS), BF16),
        ((LEN, COLS), BF16),
        ((LEN, COLS), BF16),
        ((ROWS, CH), BF16),
        ((ROWS, CH), BF16),
        ((PAD + LEN + PAD, 128), jnp.int32),
        ((NY * NC, 8, ROWS), jnp.int32),
        ((8, ROWS), jnp.int32),
        ((KB, 4 * COLS), F32),
        ((NX, NZ, KB, 4 * COLS), BF16),
        ((3, NZ, KB, CA), BF16),
        ((2, 4, KB, CA), BF16),
        ((2, 4, NX, KB, CB), BF16),
        ((3, KB, CB), BF16),
        ((NY, NC, ROWS, CH), BF16),
        ((NY, ROWS, CH), BF16),
        ((2, 2, ROWS, CH), BF16),
        *[((2, KB, COLS), F32)] * 4,
    ]
    rows = jax.ShapeDtypeStruct((ROWS, CH), BF16)
    weight = jax.ShapeDtypeStruct((2, KB, COLS), BF16)
    state = jax.ShapeDtypeStruct((2, KB, COLS), F32)
    return pl.pallas_call(
        kernel,
        name="layer",
        out_shape=(rows, rows, weight, weight, *[state] * 4),
        in_specs=[pl.BlockSpec(memory_space=pltpu.SMEM), hbm, vmem, *[hbm] * 7],
        out_specs=(vmem,) * 8,
        scratch_shapes=[pltpu.VMEM(s, t) for s, t in scratch]
        + [
            pltpu.SemaphoreType.DMA((NSEM,)),
            pltpu.SemaphoreType.DMA((NSEM,)),
            pltpu.SemaphoreType.DMA((10,)),
        ],
        compiler_params=pltpu.CompilerParams(
            collective_id=0, has_side_effects=True, vmem_limit_bytes=VMEM_LIMIT
        ),
        cost_estimate=pl.CostEstimate(flops=13 * 10**9, bytes_accessed=2**23, transcendentals=2**20),
    )(dilation, inputs, ids, fw, gw, fm, fv, gm, gv, cot)


def hand_over(*refs):
    count = len(refs) // 2
    for src, dst in zip(refs[:count], refs[count:]):
        dst[...] = src[...]


def placed(arrays):
    return pl.pallas_call(
        hand_over,
        name="hand_over",
        out_shape=tuple(jax.ShapeDtypeStruct(a.shape, a.dtype) for a in arrays),
        in_specs=[pl.BlockSpec(memory_space=pltpu.VMEM)] * len(arrays),
        out_specs=(pl.BlockSpec(memory_space=pltpu.VMEM),) * len(arrays),
    )(*arrays)


def adam_update(weight, moment, second, gradient):
    new_moment = BETA_ONE * moment + (1.0 - BETA_ONE) * gradient
    new_second = BETA_TWO * second + (1.0 - BETA_TWO) * gradient * gradient
    first_fix = 1.0 - BETA_ONE**STEP
    second_fix = 1.0 - BETA_TWO**STEP
    step_size = new_moment / first_fix / (jnp.sqrt(new_second / second_fix) + EPSILON)
    new_weight = (weight.astype(F32) - LEARN_RATE * step_size).astype(BF16)
    return (new_weight, new_moment, new_second)


def per_device(inputs, doc_ids, dilation, fw, gw, fm, fv, gm, gv, cotangent):
    results = fused(dilation, inputs[0], doc_ids, fw, gw, fm, fv, gm, gv, cotangent[0])
    layer_out, input_grad, *states = placed(results)
    return (layer_out[None], input_grad[None], *states)


def solution(mesh):
    torus = Mesh(mesh.devices.reshape(NX, NZ, NY, NC), ("x", "z", "y", "c"))
    dp, ctx = ("x", "z"), ("y", "c")
    rows, weights = P(dp, ctx, None), P(None, dp, ctx)
    return jax.shard_map(
        per_device,
        mesh=torus,
        in_specs=(rows, P(dp, ctx), P(), *[weights] * 6, rows),
        out_specs=(rows, rows, *[weights] * 6),
        check_vma=False,
    )
```

```python
import jax
import jax.numpy as jnp
from jax import lax
from jax.experimental import pallas as pl
from jax.experimental.pallas import tpu as pltpu
from jax.sharding import Mesh
from jax.sharding import PartitionSpec as P

STEP = 10
BETA_ONE = 0.9
BETA_TWO = 0.95
LEARN_RATE = 0.001
EPSILON = 1e-08

NX, NZ, NY, NC = 4, 8, 4, 2
ROWS = 128
LEN = 1024
CH = 2048
COLS = 256
KB = 64
PAD = 256
CA = 640
CB = 4 * COLS - CA
F32 = jnp.float32
BF16 = jnp.bfloat16
NSEM = 320
VMEM_LIMIT = 62 * 2**20
TR = 64
MESH = pl.DeviceIdType.MESH


def turn(position, by, size):
    return lax.rem(position + (by + size), size)


def kernel(
    dil_ref, x_in, ids_in, fw_in, gw_in, fm_in, fv_in, gm_in, gv_in, cot_in,
    lay_out, dx_out, fw_out, gw_out, fm_out, fv_out, gm_out, gv_out,
    xb, xt, wb, u0, u1, dl, dd, cotc, gcol, grow, cotv, idc, idr, idsrc,
    gsum, dw, ra, za, rb, rbx, dxb, sib, yr, fm, fv, gm, gv, ssem, rsem, lsem,
):
    x, z = lax.axis_index("x"), lax.axis_index("z")
    y, c = lax.axis_index("y"), lax.axis_index("c")
    me = y * 2 + c
    d = dil_ref[0]

    def at_x(k):
        return turn(x, k, NX)

    def at_z(k):
        return turn(z, k, NZ)

    def at_y(k):
        return turn(y, k, NY)

    oc = 1 - c
    number = {}
    sent = []

    def slot(key):
        return number.setdefault(key, len(number))

    def send(key, src, dst, dev):
        i = slot(key)
        copy = pltpu.make_async_remote_copy(
            src_ref=src, dst_ref=dst, send_sem=ssem.at[i], recv_sem=rsem.at[i],
            device_id=dev, device_id_type=MESH,
        )
        copy.start()
        sent.append(copy)

    def arrived(key, dst, dev):
        i = slot(key)
        pltpu.make_async_remote_copy(
            src_ref=dst, dst_ref=dst, send_sem=ssem.at[i], recv_sem=rsem.at[i],
            device_id=dev, device_id_type=MESH,
        ).wait_recv()

    local = []

    def bring(src, dst):
        copy = pltpu.make_async_copy(src, dst, lsem.at[len(local)])
        copy.start()
        local.append(copy)

    def rows_of(ref, block):
        return ref.at[pl.ds(pl.multiple_of(block * ROWS, ROWS), ROWS)]

    def cols_of(ref, block):
        return ref.at[:, pl.ds(pl.multiple_of(block * COLS, COLS), COLS)]

    for tap in range(2):
        bring(fw_in.at[tap], wb.at[x, z, :, pl.ds(tap * 512, COLS)])
        bring(gw_in.at[tap], wb.at[x, z, :, pl.ds(tap * 512 + COLS, COLS)])
    bring(x_in, rows_of(xb, me))
    idsrc[...] = jnp.broadcast_to(ids_in[...], (8, ROWS))

    barrier = pltpu.get_barrier_semaphore()
    ctx_peers = [
        {"y": at_y(k), "c": cc} for k in range(4) for cc in (c, oc) if (k, cc is c) != (0, True)
    ]
    peers = ctx_peers + [{"x": at_x(k)} for k in (1, 2, 3)] + [{"z": at_z(k)} for k in (1, -1)]
    for dev in peers:
        pl.semaphore_signal(barrier, inc=1, device_id=dev, device_id_type=MESH)
    pl.semaphore_wait(barrier, len(peers))
    for copy in local[:4]:
        copy.wait()

    def wa(xi, zi, lo=0, n=KB):
        return wb.at[xi, zi, pl.ds(lo, n), pl.ds(0, CA)]

    def wbp(xi, zi):
        return wb.at[xi, zi, :, pl.ds(CA, CB)]

    def half(block, h, ref=None):
        ref = xb if ref is None else ref
        return ref.at[pl.ds(pl.multiple_of(block * ROWS + h * 64, 64), 64)]

    ups = {"z": at_z(1)}
    downs = {"z": at_z(-1)}

    def z_send_a(r):
        if r < 3:
            send(("za", 1, r), wa(x, at_z(-r)), wa(x, at_z(-r)), ups)
            send(("za", -1, r), wa(x, at_z(r)), wa(x, at_z(r)), downs)
        else:
            send(("za", 1, r), wa(x, at_z(-r), 0, 32), wa(x, at_z(-r), 0, 32), ups)
            send(("za", -1, r), wa(x, at_z(r), 32, 32), wa(x, at_z(r), 32, 32), downs)

    def z_got_a(r):
        if r < 4:
            arrived(("za", 1, r - 1), wa(x, at_z(-r)), downs)
            arrived(("za", -1, r - 1), wa(x, at_z(r)), ups)
        else:
            arrived(("za", 1, r - 1), wa(x, at_z(-r), 0, 32), downs)
            arrived(("za", -1, r - 1), wa(x, at_z(r), 32, 32), ups)

    def x_send_a(r):
        for k in (1, 2, 3) if r == 4 else (1, 3):
            send(("xa", r, k), wa(x, at_z(r)), wa(x, at_z(r)), {"x": at_x(k)})

    def x_relay_a(r):
        for k, lo in ((1, 0), (3, 32)):
            arrived(("xa", r, k), wa(at_x(-k), at_z(r)), {"x": at_x(-k)})
            ref = wa(at_x(-k), at_z(r), lo, 32)
            send(("xr", r, k), ref, ref, {"x": at_x(k)})

    def x_got_a(r):
        if r == 4:
            for k in (1, 2, 3):
                arrived(("xa", r, k), wa(at_x(-k), at_z(r)), {"x": at_x(-k)})
        else:
            for k, lo in ((1, 0), (3, 32)):
                arrived(("xr", r, k), wa(at_x(2), at_z(r), lo, 32), {"x": at_x(-k)})

    def carried(direction, r):
        return (0, 1, 2, 3) if r < 4 else ((0, 1) if direction > 0 else (2, 3))

    def z_send_b(r, k):
        for s, dev in ((1, ups), (-1, downs)):
            if k in carried(s, r + 1):
                ref = wbp(at_x(k), at_z(-s * r))
                send(("zb", s, r, k), ref, ref, dev)

    def z_got_b(r, k):
        for s, dev in ((1, downs), (-1, ups)):
            if k in carried(s, r):
                arrived(("zb", s, r - 1, k), wbp(at_x(k), at_z(-s * r)), dev)

    z_send_a(0)
    for k in (1, 2, 3):
        send(("xb", k), wbp(x, z), wbp(x, z), {"x": at_x(k)})
    local[4].wait()
    for s, h in ((1, 0), (-1, 1)):
        send(("X", s, 0), half(me, h), half(me, h), {"y": at_y(s)})
    send(("Xc", 0), rows_of(xb, me), rows_of(xb, me), {"c": oc})
    z_send_b(0, 0)
    x_send_a(0)
    for s, h in ((1, 1), (-1, 0)):
        send(("X", s, 1), half(me, h), half(me, h), {"y": at_y(s)})
    ctx_offsets = [(k, o) for k in range(4) for o in (0, 1) if (k, o) != (0, 0)]

    def ctx_dev(k, o):
        return {"y": at_y(k), "c": turn(c, o, NC)}

    def ctx_id(k, o):
        return at_y(k) * 2 + turn(c, o, NC)

    for k, o in ctx_offsets:
        send(("id", k, o), idsrc, idr.at[me], ctx_dev(k, o))

    bring(cot_in, cotv)
    for src, dst in ((fm_in, fm), (fv_in, fv), (gm_in, gm), (gv_in, gv)):
        bring(src, dst)
    states = local[6:]
    idr[me] = idsrc[...]
    idc[pl.ds(0, PAD)] = jnp.full((PAD, 128), -1, jnp.int32)
    idc[pl.ds(PAD + LEN, PAD)] = jnp.full((PAD, 128), -2, jnp.int32)
    u1[:, pl.ds(0, PAD)] = jnp.zeros((4, PAD, 128), F32)
    dl[:, pl.ds(LEN, PAD)] = jnp.zeros((4, PAD, 128), F32)

    def transposed(block):
        rows = pl.ds(pl.multiple_of(block * ROWS, ROWS), ROWS)

        @pl.loop(0, NX)
        def _(xi):
            part = xb[rows, pl.ds(pl.multiple_of(xi * 512, 512), 512)]
            xt[xi, :, :, rows] = part.T.reshape(NZ, KB, ROWS)

    z_got_a(1)
    z_send_a(1)
    for r in (1, -1):
        x_send_a(r)
    for k in (1, 2, 3):
        arrived(("xb", k), wbp(at_x(-k), z), {"x": at_x(-k)})
        z_send_b(0, 4 - k)
    z_got_b(1, 0)
    z_send_b(1, 0)
    x_relay_a(0)
    transposed(me)
    arrived(("X", 1, 0), half(at_y(-1) * 2 + c, 0), {"y": at_y(-1)})
    send(("X", 1, 2), half(at_y(-1) * 2 + c, 0), half(at_y(-1) * 2 + c, 0), {"y": at_y(1)})
    arrived(("X", -1, 0), half(at_y(1) * 2 + c, 1), {"y": at_y(1)})
    send(("X", -1, 2), half(at_y(1) * 2 + c, 1), half(at_y(1) * 2 + c, 1), {"y": at_y(-1)})
    z_got_a(2)
    z_send_a(2)
    for r in (2, -2):
        x_send_a(r)
    local[5].wait()
    for k, o in ctx_offsets:
        send(("cot", k, o), cols_of(cotv, ctx_id(k, o)), rows_of(cotc, me), ctx_dev(k, o))
    for part in range(2):
        rows = pl.ds(pl.multiple_of(me * ROWS + part * 64, 64), 64)
        cotc[rows] = cotv[pl.ds(part * 64, 64), pl.ds(pl.multiple_of(me * COLS, COLS), COLS)]
    arrived(("Xc", 0), rows_of(xb, y * 2 + oc), {"c": oc})
    transposed(y * 2 + oc)
    for r in (1, -1):
        x_relay_a(r)
    for k in (3, 2, 1):
        z_got_b(1, k)
        z_send_b(1, k)
    arrived(("X", 1, 1), half(at_y(-1) * 2 + c, 1), {"y": at_y(-1)})
    send(("Xc", 1), rows_of(xb, at_y(-1) * 2 + c), rows_of(xb, at_y(-1) * 2 + c), {"c": oc})
    arrived(("X", -1, 1), half(at_y(1) * 2 + c, 0), {"y": at_y(1)})
    send(("Xc", 2), rows_of(xb, at_y(1) * 2 + c), rows_of(xb, at_y(1) * 2 + c), {"c": oc})
    z_got_a(3)
    z_send_a(3)
    for r in (3, -3):
        x_send_a(r)
    z_got_b(2, 0)
    z_send_b(2, 0)
    transposed(at_y(-1) * 2 + c)
    z_got_b(2, 3)
    z_send_b(2, 3)
    for r in (2, -2):
        x_relay_a(r)
    transposed(at_y(1) * 2 + c)
    for k in (2, 1):
        z_got_b(2, k)
        z_send_b(2, k)
    z_got_a(4)
    x_send_a(4)
    arrived(("Xc", 1), rows_of(xb, at_y(-1) * 2 + oc), {"c": oc})
    transposed(at_y(-1) * 2 + oc)
    arrived(("Xc", 2), rows_of(xb, at_y(1) * 2 + oc), {"c": oc})
    transposed(at_y(1) * 2 + oc)
    z_got_b(3, 0)
    z_send_b(3, 0)
    z_got_b(3, 3)
    z_send_b(3, 3)
    for r in (3, -3):
        x_relay_a(r)
    arrived(("X", 1, 2), half(at_y(2) * 2 + c, 0), {"y": at_y(-1)})
    arrived(("X", -1, 2), half(at_y(2) * 2 + c, 1), {"y": at_y(1)})
    send(("Xc", 3), rows_of(xb, at_y(2) * 2 + c), rows_of(xb, at_y(2) * 2 + c), {"c": oc})
    for k in (2, 1):
        z_got_b(3, k)
        z_send_b(3, k)
    transposed(at_y(2) * 2 + c)
    for k, o in ctx_offsets:
        arrived(("id", k, o), idr.at[ctx_id(-k, o)], ctx_dev(-k, o))

    @pl.loop(0, NY * NC)
    def _(block):
        spread = jnp.broadcast_to(idr[block, 0:1, :], (ROWS, ROWS))
        idc[pl.ds(pl.multiple_of(PAD + block * ROWS, ROWS), ROWS)] = spread.T

    arrived(("Xc", 3), rows_of(xb, at_y(2) * 2 + oc), {"c": oc})
    transposed(at_y(2) * 2 + oc)

    def forward(pair, first):
        @pl.loop(0, 1)
        def _(i):
            rows = pl.ds(pl.multiple_of(i * 1024, 512), 1024)
            lags = pl.ds(pl.multiple_of(PAD + i * 1024, 256), 1024)
            lhs = jnp.concatenate(
                [
                    xb[rows, pl.ds(pl.multiple_of(xi * 512 + pair * 128, 128), 128)]
                    for xi in range(NX)
                ],
                axis=1,
            )
            w0 = wb[:, pl.ds(pair * 2, 2), :, pl.ds(0, 512)].reshape(512, 512)
            w1 = wb[:, pl.ds(pair * 2, 2), :, pl.ds(512, 512)].reshape(512, 512)
            p0 = jnp.dot(lhs, w0, preferred_element_type=F32)
            p1 = jnp.dot(lhs, w1, preferred_element_type=F32)
            u0[rows] = p0 if first else u0[rows] + p0
            for j in range(4):
                part = p1[:, j * 128 : j * 128 + 128]
                u1[j, lags] = part if first else u1[j, lags] + part

    pair = z // 2
    lean = 1 - 2 * lax.rem(z, 2)
    for r in (0, 1, -1):
        x_got_a(r)
    forward(pair, True)
    for r in (2, -2):
        x_got_a(r)
    forward(turn(pair, -lean, 4), False)
    for r in (3, -3):
        x_got_a(r)
    forward(turn(pair, lean, 4), False)
    x_got_a(4)
    for k in range(4):
        z_got_b(4, k)
    forward(turn(pair, 2, 4), False)
    for k, o in ctx_offsets:
        arrived(("cot", k, o), rows_of(cotc, ctx_id(-k, o)), ctx_dev(-k, o))

    @pl.loop(0, LEN // TR)
    def _(i):
        t0 = pl.multiple_of(i * TR, TR)
        same = idc[pl.ds(PAD + t0, TR)] == idc[pl.ds(PAD + t0 - d, TR)]
        for j in range(2):
            pre = []
            for part in range(2):
                cols = pl.ds(part * COLS + j * 128, 128)
                lag = u1[part * 2 + j, pl.ds(PAD + t0 - d, TR)]
                pre.append(u0[pl.ds(t0, TR), cols] + jnp.where(same, lag, 0.0))
            f = jnp.tanh(pre[0])
            g = 0.5 * jnp.tanh(0.5 * pre[1]) + 0.5
            near = pl.ds(j * 128, 128)
            far = pl.ds(COLS + j * 128, 128)
            gcol[pl.ds(t0, TR), near] = (f * g).astype(BF16)
            cot = cotc[pl.ds(t0, TR), near].astype(F32) * g
            fd = (cot * (1.0 - f * f)).astype(BF16)
            gd = (cot * f * (1.0 - g)).astype(BF16)
            dd[pl.ds(t0, TR), near] = fd
            dd[pl.ds(t0, TR), far] = gd
            dl[j, pl.ds(t0, TR)] = fd.astype(F32)
            dl[2 + j, pl.ds(t0, TR)] = gd.astype(F32)

    for k, o in ctx_offsets:
        send(("gat", k, o), rows_of(gcol, ctx_id(k, o)), cols_of(grow, me), ctx_dev(k, o))
    for part in range(2):
        rows = pl.ds(pl.multiple_of(me * ROWS + part * 64, 64), 64)
        grow[pl.ds(part * 64, 64), pl.ds(pl.multiple_of(me * COLS, COLS), COLS)] = gcol[rows]

    @pl.loop(0, LEN // TR)
    def _(i):
        t0 = pl.multiple_of(i * TR, TR)
        same = idc[pl.ds(PAD + t0, TR)] == idc[pl.ds(PAD + t0 + d, TR)]
        for j in range(4):
            ahead = dl[j, pl.ds(t0 + d, TR)]
            dd[pl.ds(t0, TR), pl.ds(512 + j * 128, 128)] = jnp.where(same, ahead, 0.0).astype(BF16)

    def grad_w(*steps):
        for part in range(2):
            cols = pl.ds(part * 512, 512)
            lhs = [xt[:, at_z(r)].reshape(NX * KB, LEN) for r in steps]
            out = jnp.dot(jnp.concatenate(lhs, axis=0), dd[:, cols], preferred_element_type=F32)
            for i, r in enumerate(steps):
                mine = out[i * 256 : i * 256 + 256].astype(BF16)
                dw[:, at_z(r), :, cols] = mine.reshape(NX, KB, 512)

    def da(xi, zi, lo=0, n=KB):
        return dw.at[xi, zi, pl.ds(lo, n), pl.ds(0, CA)]

    def db(xi, zi):
        return dw.at[xi, zi, :, pl.ds(CA, CB)]

    def direct(r):
        return r == 4

    def sum_x_send(r):
        zi = at_z(r)
        if direct(r):
            for k in (1, 2, 3):
                send(("sxa", r, k), da(at_x(k), zi), ra.at[k - 1, zi], {"x": at_x(k)})
        else:
            for k, lo in ((1, 0), (3, 32)):
                dst = ra.at[1, zi, pl.ds(lo, 32)]
                send(("sxr", r, k), da(at_x(2), zi, lo, 32), dst, {"x": at_x(k)})

    def sum_x_relay(r):
        zi = at_z(r)
        for k, lo in ((1, 0), (3, 32)):
            rows = pl.ds(lo, 32)
            arrived(("sxr", r, k), ra.at[1, zi, rows], {"x": at_x(-k)})
            ref = da(at_x(k), zi, lo, 32)
            ref[...] = (ref[...].astype(F32) + ra[1, zi, rows].astype(F32)).astype(BF16)
            send(("sxa", r, k), da(at_x(k), zi), ra.at[k - 1, zi], {"x": at_x(k)})

    def sum_x_got(r):
        for k in (1, 2, 3) if direct(r) else (1, 3):
            arrived(("sxa", r, k), ra.at[k - 1, at_z(r)], {"x": at_x(-k)})

    def a_sum(r):
        zi = at_z(r)
        total = da(x, zi)[...].astype(F32) + ra[0, zi].astype(F32) + ra[2, zi].astype(F32)
        return total + ra[1, zi].astype(F32) if direct(r) else total

    def a_far():
        sum_x_got(4)
        da(x, at_z(4))[...] = a_sum(4).astype(BF16)
        send(("sza", 1, 4), da(x, at_z(4), 0, 32), za.at[0, 3, pl.ds(0, 32)], ups)
        send(("sza", -1, 4), da(x, at_z(-4), 32, 32), za.at[1, 3, pl.ds(32, 32)], downs)

    def a_step(r):
        for s, h, dev, src in ((1, 0, ups, downs), (-1, 1, downs, ups)):
            sum_x_got(s * r)
            total = a_sum(s * r)
            ref = da(x, at_z(s * r))
            if r == 3:
                lo = pl.ds(h * 32, 32)
                arrived(("sza", s, r + 1), za.at[h, r, lo], src)
                ref[...] = total.astype(BF16)
                part = total[h * 32 : h * 32 + 32] + za[h, r, lo].astype(F32)
                da(x, at_z(s * r), h * 32, 32)[...] = part.astype(BF16)
            else:
                arrived(("sza", s, r + 1), za.at[h, r], src)
                ref[...] = (total + za[h, r].astype(F32)).astype(BF16)
            send(("sza", s, r), ref, za.at[h, r - 1], dev)

    def b_far():
        for s, h, dev in ((1, 0, ups), (-1, 1, downs)):
            for k in carried(s, 4):
                send(("szb", s, 4, k), db(at_x(k), at_z(s * 4)), rb.at[h, 3, k], dev)

    def b_step(r, k):
        for s, h, dev, src in ((1, 0, ups, downs), (-1, 1, downs, ups)):
            ref = db(at_x(k), at_z(s * r))
            if k in carried(s, r + 1):
                arrived(("szb", s, r + 1, k), rb.at[h, r, k], src)
                ref[...] = (ref[...].astype(F32) + rb[h, r, k].astype(F32)).astype(BF16)
            send(("szb", s, r, k), ref, rb.at[h, r - 1, k], dev)

    def b_last(k):
        for s, h, src in ((1, 0, downs), (-1, 1, ups)):
            arrived(("szb", s, 1, k), rb.at[h, 0, k], src)
        ref = db(at_x(k), z)
        total = ref[...].astype(F32) + (rb[0, 0, k].astype(F32) + rb[1, 0, k].astype(F32))
        if k == 0:
            gsum[:, pl.ds(CA, CB)] = total
        else:
            ref[...] = total.astype(BF16)
            send(("sxb", k), ref, rbx.at[k - 1], {"x": at_x(k)})

    def grad_x(k):
        yi = at_y(k)
        lhs = dd[pl.ds(pl.multiple_of(yi * 256, 256), 256), :]

        @pl.loop(0, NX)
        def _(xi):
            out = lax.dot_general(
                lhs, wb[xi].reshape(512, 1024), (((1,), (1,)), ((), ())), preferred_element_type=F32
            )
            out = out.astype(BF16).reshape(NC, ROWS, 512)
            dxb[yi, :, :, pl.ds(pl.multiple_of(xi * 512, 512), 512)] = out

        send(("sib", k), dxb.at[yi, oc], sib.at[yi], {"c": oc})

    def pair_sum(k):
        yi = at_y(k)
        arrived(("sib", k), sib.at[yi], {"c": oc})

        @pl.loop(0, 4)
        def _(i):
            rows = pl.ds(pl.multiple_of(i * 32, 32), 32)
            total = dxb[yi, c, rows].astype(F32) + sib[yi, rows].astype(F32)
            dxb[yi, c, rows] = total.astype(BF16)

    def y_far():
        pair_sum(2)
        for s, h in ((1, 0), (-1, 1)):
            rows = pl.ds(h * 64, 64)
            send(("y", s, 2), dxb.at[at_y(2), c, rows], yr.at[h, 0, rows], {"y": at_y(s)})

    def y_step():
        for s, h in ((1, 0), (-1, 1)):
            pair_sum(s)
            rows = pl.ds(h * 64, 64)
            yi = at_y(s)
            arrived(("y", s, 2), yr.at[h, 0, rows], {"y": at_y(-s)})

            @pl.loop(0, 2)
            def _(i):
                some = pl.ds(pl.multiple_of(h * 64 + i * 32, 32), 32)
                total = dxb[yi, c, some].astype(F32) + yr[h, 0, some].astype(F32)
                dxb[yi, c, some] = total.astype(BF16)

            send(("y", s, 1), dxb.at[yi, c], yr.at[h, 1], {"y": at_y(s)})

    def adam(j):
        tap, gate, cols = j // 4, (j // 2) % 2, pl.ds((j % 2) * 128, 128)
        moment, second = ((fm, fv), (gm, gv))[gate]
        outs = ((fw_out, fm_out, fv_out), (gw_out, gm_out, gv_out))[gate]
        results = adam_update(
            wb[x, z, :, pl.ds(j * 128, 128)],
            moment[tap, :, cols],
            second[tap, :, cols],
            gsum[:, pl.ds(j * 128, 128)] * (1.0 / (LEN * NX * NZ)),
        )
        for out, result in zip(outs, results):
            out[tap, :, cols] = result

    def y_last():
        pair_sum(0)
        for s, h in ((1, 0), (-1, 1)):
            arrived(("y", s, 1), yr.at[h, 1], {"y": at_y(-s)})

        @pl.loop(0, 4)
        def _(i):
            rows = pl.ds(pl.multiple_of(i * 32, 32), 32)
            far = yr[0, 1, rows].astype(F32) + yr[1, 1, rows].astype(F32)
            back = dxb[y, c, rows].astype(F32) + far
            dx_out[rows] = (cotv[rows].astype(F32) + back).astype(BF16)

    def a_last():
        sum_x_got(0)
        total = a_sum(0)
        for s, h, src in ((1, 0, downs), (-1, 1, ups)):
            arrived(("sza", s, 1), za.at[h, 0], src)
        gsum[:, pl.ds(0, CA)] = total + (za[0, 0].astype(F32) + za[1, 0].astype(F32))
        for j in range(CA // 128):
            adam(j)

    def b_end():
        for k in (1, 2, 3):
            arrived(("sxb", k), rbx.at[k - 1], {"x": at_x(-k)})
        across = rbx[0].astype(F32) + rbx[1].astype(F32) + rbx[2].astype(F32)
        gsum[:, pl.ds(CA, CB)] += across
        for j in range(CA // 128, 8):
            adam(j)

    grad_w(4)
    sum_x_send(4)
    b_far()
    grad_x(2)
    grad_w(3, -3)
    sum_x_send(3)
    sum_x_send(-3)
    grad_w(2)
    sum_x_send(2)
    for k in range(4):
        b_step(3, k)
    grad_w(-2)
    sum_x_send(-2)
    a_far()
    y_far()
    grad_x(1)
    for r in (3, -3):
        sum_x_relay(r)
    grad_w(1, -1)
    sum_x_send(1)
    sum_x_send(-1)
    for k in range(4):
        b_step(2, k)
    for r in (2, -2):
        sum_x_relay(r)
    grad_x(-1)
    grad_w(0)
    sum_x_send(0)
    a_step(3)
    y_step()
    for k in range(4):
        b_step(1, k)
    for r in (1, -1, 0):
        sum_x_relay(r)
    grad_x(0)
    a_step(2)
    for k, o in ctx_offsets:
        arrived(("gat", k, o), cols_of(grow, ctx_id(-k, o)), ctx_dev(-k, o))

    @pl.loop(0, 4)
    def _(i):
        rows = pl.ds(pl.multiple_of(i * 32, 32), 32)
        mine = xb[pl.ds(pl.multiple_of(me * ROWS + i * 32, 32), 32)]
        lay_out[rows] = (mine.astype(F32) + grow[rows].astype(F32)).astype(BF16)

    for k in (1, 2, 3, 0):
        b_last(k)
    a_step(1)
    for copy in states:
        copy.wait()
    y_last()
    b_end()
    a_last()
    for copy in sent:
        copy.wait_send()


def fused(dilation, inputs, ids, fw, gw, fm, fv, gm, gv, cot):
    hbm = pl.BlockSpec(memory_space=pltpu.HBM)
    vmem = pl.BlockSpec(memory_space=pltpu.VMEM)
    scratch = [
        ((LEN, CH), BF16),
        ((NX, NZ, KB, LEN), BF16),
        ((NX, NZ, KB, 4 * COLS), BF16),
        ((LEN, 2 * COLS), F32),
        ((4, PAD + LEN, 128), F32),
        ((4, LEN + PAD, 128), F32),
        ((LEN, 4 * COLS), BF16),
        ((LEN, COLS), BF16),
        ((LEN, COLS), BF16),
        ((ROWS, CH), BF16),
        ((ROWS, CH), BF16),
        ((PAD + LEN + PAD, 128), jnp.int32),
        ((NY * NC, 8, ROWS), jnp.int32),
        ((8, ROWS), jnp.int32),
        ((KB, 4 * COLS), F32),
        ((NX, NZ, KB, 4 * COLS), BF16),
        ((3, NZ, KB, CA), BF16),
        ((2, 4, KB, CA), BF16),
        ((2, 4, NX, KB, CB), BF16),
        ((3, KB, CB), BF16),
        ((NY, NC, ROWS, CH), BF16),
        ((NY, ROWS, CH), BF16),
        ((2, 2, ROWS, CH), BF16),
        *[((2, KB, COLS), F32)] * 4,
    ]
    rows = jax.ShapeDtypeStruct((ROWS, CH), BF16)
    weight = jax.ShapeDtypeStruct((2, KB, COLS), BF16)
    state = jax.ShapeDtypeStruct((2, KB, COLS), F32)
    return pl.pallas_call(
        kernel,
        name="layer",
        out_shape=(rows, rows, weight, weight, *[state] * 4),
        in_specs=[pl.BlockSpec(memory_space=pltpu.SMEM), hbm, vmem, *[hbm] * 7],
        out_specs=(vmem,) * 8,
        scratch_shapes=[pltpu.VMEM(s, t) for s, t in scratch]
        + [
            pltpu.SemaphoreType.DMA((NSEM,)),
            pltpu.SemaphoreType.DMA((NSEM,)),
            pltpu.SemaphoreType.DMA((10,)),
        ],
        compiler_params=pltpu.CompilerParams(
            collective_id=0, has_side_effects=True, vmem_limit_bytes=VMEM_LIMIT
        ),
        cost_estimate=pl.CostEstimate(flops=13 * 10**9, bytes_accessed=2**23, transcendentals=2**20),
    )(dilation, inputs, ids, fw, gw, fm, fv, gm, gv, cot)


def hand_over(*refs):
    count = len(refs) // 2
    for src, dst in zip(refs[:count], refs[count:]):
        dst[...] = src[...]


def placed(arrays):
    return pl.pallas_call(
        hand_over,
        name="hand_over",
        out_shape=tuple(jax.ShapeDtypeStruct(a.shape, a.dtype) for a in arrays),
        in_specs=[pl.BlockSpec(memory_space=pltpu.VMEM)] * len(arrays),
        out_specs=(pl.BlockSpec(memory_space=pltpu.VMEM),) * len(arrays),
    )(*arrays)


def adam_update(weight, moment, second, gradient):
    new_moment = BETA_ONE * moment + (1.0 - BETA_ONE) * gradient
    new_second = BETA_TWO * second + (1.0 - BETA_TWO) * gradient * gradient
    first_fix = 1.0 - BETA_ONE**STEP
    second_fix = 1.0 - BETA_TWO**STEP
    step_size = new_moment / first_fix / (jnp.sqrt(new_second / second_fix) + EPSILON)
    new_weight = (weight.astype(F32) - LEARN_RATE * step_size).astype(BF16)
    return (new_weight, new_moment, new_second)


def per_device(inputs, doc_ids, dilation, fw, gw, fm, fv, gm, gv, cotangent):
    results = fused(dilation, inputs[0], doc_ids, fw, gw, fm, fv, gm, gv, cotangent[0])
    layer_out, input_grad, *states = placed(results)
    return (layer_out[None], input_grad[None], *states)


def solution(mesh):
    torus = Mesh(mesh.devices.reshape(NX, NZ, NY, NC), ("x", "z", "y", "c"))
    dp, ctx = ("x", "z"), ("y", "c")
    rows, weights = P(dp, ctx, None), P(None, dp, ctx)
    return jax.shard_map(
        per_device,
        mesh=torus,
        in_specs=(rows, P(dp, ctx), P(), *[weights] * 6, rows),
        out_specs=(rows, rows, *[weights] * 6),
        check_vma=False,
    )
```
